128 devices in a mesh: seq: 16 (over z, x), grp: 8 (over y, core).
Axes of the slice: x: 4, y: 4, z: 4, core: 2. Of those that a mesh axis runs over, the one named last changes fastest.
Arguments:
- query: bfloat16 [512, 24576], P(('grp', 'seq')), parts along dimension 0
- dec_query: bfloat16 [128, 24576], P(('grp', 'seq')), parts along dimension 0
- cache_kv: bfloat16 [131072, 576], P(('grp', 'seq')), parts along dimension 0
- span_kv: bfloat16 [512, 576], P(('grp', 'seq')), parts along dimension 0, may hold values from -4 to 4
- dec_kv: bfloat16 [128, 576], P(('grp', 'seq')), parts along dimension 0
- cache_fill: int32 [128], P('grp'), parts along dimension 0, may hold values from 128 to 960, as said below
- owner: int32 [512], P('grp'), parts along dimension 0, may hold values from 0 to 15, as said below
- slot: int32 [512], P('grp'), parts along dimension 0, may hold values from 128 to 1023, as said below
- dec_len: int32 [128], P('grp'), parts along dimension 0, may hold values from 1 to 64
- w_uk: bfloat16 [128, 128, 512], P('seq'), may hold values from -0.5 to 0.5
- w_uv: bfloat16 [128, 512, 128], P('seq'), may hold values from -0.25 to 0.25
Outputs:
- span_out: bfloat16 [512, 16384], P('grp', 'seq'), parts along dimension 0
- dec_out: bfloat16 [128, 16384], P('grp', 'seq'), parts along dimension 0
- new_cache: bfloat16 [131072, 576], P(('grp', 'seq')), parts along dimension 0
The draws below stay inside these ranges and needn't reach their ends.
There are 8 independent parts, one for each index of `grp`. The reference program is written for one: setup_inputs(seed, part) draws one part's arguments, and reference() takes and returns one part's arrays. A program takes and returns all parts, laid end to end along the dimension named above; an argument that names none is the same for every part. Nothing has to cross between parts.
Inputs may be any that keep to these rules, and one draw needn't show every extreme that they name: `cache_fill`: every block keeps at least 128 filled slots and room for all 64 new rows. `owner`: a block index for each prefill token; blocks receive unequal numbers of rows. slot[t] = cache_fill[owner[t]] plus the number of earlier prefill tokens with the same owner.
All inputs are finite; a program needn't handle non-finite values.
Results may differ from the reference program's by a relative error of at most 0.014.
Values may be sent and summed in bfloat16 or wider, within the bound.
A program may use at most 192 MiB of HBM per device.

```python
import jax
import jax.numpy as jnp
from jax import lax

H = 128
DN = 128
DR = 64
DC = 512
DV = 128
POS_DEV = 1024
SPAN = 64
ROWS = 16
CACHE = 16384
N_SEQ = 16


def decode_rope(key):
    return jax.random.normal(jax.random.fold_in(key, 901), (ROWS, DR), jnp.float32)


def placement_draw(key):
    key = jax.random.fold_in(key, 500)
    fill = jax.random.randint(jax.random.fold_in(key, 1), (N_SEQ,), POS_DEV // 8, POS_DEV - SPAN + 1)
    weights = jax.random.randint(jax.random.fold_in(key, 2), (N_SEQ,), 1, 9)
    cumul = jnp.cumsum(weights)
    pick = jax.random.randint(jax.random.fold_in(key, 3), (SPAN,), 0, cumul[N_SEQ - 1])
    owner = jnp.sum((cumul[None, :] <= pick[:, None]).astype(jnp.int32), axis=1).astype(jnp.int32)
    onehot = (owner[:, None] == jnp.arange(N_SEQ, dtype=jnp.int32)[None, :]).astype(jnp.int32)
    earlier = jnp.cumsum(onehot, axis=0) - onehot
    rank = jnp.sum(earlier * onehot, axis=1)
    base = jnp.sum(onehot * fill[None, :], axis=1)
    return (fill.astype(jnp.int32), owner, (base + rank).astype(jnp.int32))


def draw_cache_fill(key, part):
    return placement_draw(key)[0]


def draw_owner(key, part):
    return placement_draw(key)[1]


def draw_slot(key, part):
    return placement_draw(key)[2]


def draw_query(key, part):
    key = jax.random.fold_in(key, 1)
    values = jax.random.normal(key, (SPAN, H, DN + DR), jnp.float32)
    return values.reshape(SPAN, H * (DN + DR)).astype(jnp.bfloat16)


def draw_dec_query(key, part):
    shared = decode_rope(key)
    key = jax.random.fold_in(key, 2)
    values = jax.random.normal(key, (ROWS, H, DN + DR), jnp.float32)
    rope = 1.1 * shared[:, None, :] + 0.5 * values[:, :, DN:]
    values = jnp.concatenate([values[:, :, :DN], rope], axis=2)
    return values.reshape(ROWS, H * (DN + DR)).astype(jnp.bfloat16)


def draw_dec_kv(key, part):
    shared = decode_rope(key)
    key = jax.random.fold_in(key, 3)
    latent = 0.5 * jax.random.normal(key, (ROWS, DC), jnp.float32)
    return jnp.concatenate([latent, shared], axis=1).astype(jnp.bfloat16)


def draw_cache_kv(key, part):
    key = jax.random.fold_in(key, 4)
    values = jax.random.normal(key, (CACHE, DC + DR), jnp.float32)
    latent = 0.5 * values[:, :DC]
    rope = values[:, DC:]
    return jnp.concatenate([latent, rope], axis=1).astype(jnp.bfloat16)


def touch_ends(values, key, low, high):
    longest = values.shape.index(max(values.shape))
    spots = []
    for shift in (0, 1):
        where = [jax.random.randint(jax.random.fold_in(key, axis), (), 0, length) for axis, length in enumerate(values.shape)]
        where[longest] = (where[longest] + shift) % values.shape[longest]
        spots.append(tuple(where))
    return values.at[spots[0]].set(low).at[spots[1]].set(high)


def block_levels(key, extent, pieces, low, high):
    def one(position, shards_of):
        steps = jax.random.uniform(jax.random.fold_in(jax.random.fold_in(key, 6), position), (shards_of,), jnp.float32, low / len(pieces), high / len(pieces))
        return jnp.repeat(jnp.exp(steps), extent[position] // shards_of).reshape((-1,) + (1,) * (len(extent) - position - 1))

    loudness = one(*pieces[0])
    for cut in pieces[1:]:
        loudness = loudness * one(*cut)
    return loudness


def gaussian(rng, extent, spread, most, cuts=(), kind=jnp.bfloat16):
    drawn = jax.random.normal(rng, extent, jnp.float32) * spread
    if len(cuts) > 0:
        drawn = block_levels(rng, extent, cuts, -0.22, 0.18) * drawn
    return jnp.clip(drawn, min=-most, max=most).astype(kind)


def setup_inputs(seed: int = 0, part: int = 0) -> dict:
    key_of = jax.random.split(jax.random.key(seed), 12)
    own_keys = jax.random.split(jax.random.fold_in(key_of[11], part), 12)
    query = draw_query(jax.random.fold_in(jax.random.fold_in(key_of[11], part), 71), part)
    dec_query = draw_dec_query(jax.random.fold_in(jax.random.fold_in(key_of[11], part), 71), part)
    cache_kv = draw_cache_kv(jax.random.fold_in(jax.random.fold_in(key_of[11], part), 71), part)
    span_kv = gaussian(own_keys[3], (SPAN, DC + DR), 0.5, 4.0, ((0, 16),))
    dec_kv = draw_dec_kv(jax.random.fold_in(jax.random.fold_in(key_of[11], part), 71), part)
    cache_fill = draw_cache_fill(jax.random.fold_in(jax.random.fold_in(key_of[11], part), 71), part)
    owner = draw_owner(jax.random.fold_in(jax.random.fold_in(key_of[11], part), 71), part)
    slot = draw_slot(jax.random.fold_in(jax.random.fold_in(key_of[11], part), 71), part)
    dec_len = touch_ends(jax.random.randint(own_keys[8], (ROWS,), 1, SPAN + 1), jax.random.fold_in(own_keys[8], 1), 1, SPAN).astype(jnp.int32)
    w_uk = gaussian(key_of[9], (H, DN, DC), DN ** -0.5, 0.5, ((0, 16),))
    w_uv = gaussian(key_of[10], (H, DC, DV), DC ** -0.5, 0.25, ((0, 16),))
    return {"query": query, "dec_query": dec_query, "cache_kv": cache_kv, "span_kv": span_kv, "dec_kv": dec_kv, "cache_fill": cache_fill, "owner": owner, "slot": slot, "dec_len": dec_len, "w_uk": w_uk, "w_uv": w_uv}


score_scale = 0.1353


def tag_rows(rows, cache_fill, owner, slot, pos_dev, span):
    block = rows // pos_dev
    local = rows % pos_dev
    count = cache_fill.shape[0]
    fills = jnp.sum(jnp.where(block[:, None] == jnp.arange(count, dtype=jnp.int32)[None, :], cache_fill[None, :], 0), axis=1)
    base = jnp.where(local < fills, -1, span + 1)
    target = owner * pos_dev + slot
    token = jnp.arange(span, dtype=jnp.int32)
    placed = jnp.sum(jnp.where(rows[:, None] == target[None, :], token[None, :] + 1, 0), axis=1)
    return jnp.where(placed > 0, placed - 1, base).astype(jnp.int32)


def combine(state, peak, total, output):
    old_peak, old_total, old_acc = state
    top = jnp.maximum(old_peak, peak)
    keep = jnp.exp(old_peak - top)
    fresh = jnp.exp(peak - top)
    return top, old_total * keep + total * fresh, old_acc * keep[..., None] + output * fresh[..., None]


def block_partial(absorbed, keys, tags, limits):
    scores = jnp.einsum("qhc,pc->qhp", absorbed.astype(jnp.float32), keys.astype(jnp.float32)) * score_scale
    visible = tags[None, None, :] < limits[:, None, None]
    peak = jnp.max(jnp.where(visible, scores, -1e30), axis=2)
    weights = jnp.where(visible, jnp.exp(scores - peak[..., None]), 0.0)
    total = jnp.sum(weights, axis=2)
    rounded = lax.optimization_barrier(weights.astype(jnp.bfloat16)).astype(jnp.float32)
    output = jnp.einsum("qhp,pc->qhc", rounded, keys[:, :DC].astype(jnp.float32))
    return peak, total, output


def absorb(query, w_uk):
    shaped = query.reshape(query.shape[0], H, DN + DR)
    latent = jnp.einsum("thn,hnc->thc", shaped[:, :, :DN].astype(jnp.float32), w_uk.astype(jnp.float32)).astype(jnp.bfloat16)
    return jnp.concatenate([latent, shaped[:, :, DN:]], axis=2)


def reference(query, dec_query, cache_kv, span_kv, dec_kv, cache_fill, owner, slot, dec_len, w_uk, w_uv):
    index = (owner * POS_DEV + slot).astype(jnp.int32)
    new_cache = cache_kv.at[index].set(span_kv)
    tags = tag_rows(jnp.arange(CACHE, dtype=jnp.int32), cache_fill, owner, slot, POS_DEV, SPAN)
    absorbed = jnp.concatenate([absorb(query, w_uk), absorb(dec_query, w_uk)], axis=0)
    limits = jnp.concatenate([jnp.arange(1, SPAN + 1, dtype=jnp.int32), dec_len.astype(jnp.int32)])
    count = SPAN + ROWS
    init = (jnp.full((count, H), -1e30, jnp.float32), jnp.zeros((count, H), jnp.float32), jnp.zeros((count, H, DC), jnp.float32))

    def step(carry, block):
        start = (block * POS_DEV).astype(jnp.int32)
        keys = lax.dynamic_slice_in_dim(new_cache, start, POS_DEV, 0)
        block_tags = lax.dynamic_slice_in_dim(tags, start, POS_DEV, 0)
        return combine(carry, *block_partial(absorbed, keys, block_tags, limits)), None

    (peak, total, acc), unused = lax.scan(step, init, jnp.arange(N_SEQ, dtype=jnp.int32))
    dec_abs = absorbed[SPAN:].astype(jnp.float32)
    own = jnp.einsum("rhc,rc->rh", dec_abs, dec_kv.astype(jnp.float32)) * score_scale
    own_out = jnp.broadcast_to(dec_kv[:, None, :DC].astype(jnp.float32), (ROWS, H, DC))
    dec_state = combine((peak[SPAN:], total[SPAN:], acc[SPAN:]), own, jnp.ones((ROWS, H), jnp.float32), own_out)
    total = jnp.concatenate([total[:SPAN], dec_state[1]], axis=0)
    acc = jnp.concatenate([acc[:SPAN], dec_state[2]], axis=0)
    latent_out = (acc / total[..., None]).astype(jnp.bfloat16)
    result = jnp.einsum("qhc,hcv->qhv", latent_out.astype(jnp.float32), w_uv.astype(jnp.float32)).astype(jnp.bfloat16)
    result = result.reshape(count, H * DV)
    return result[:SPAN], result[SPAN:], new_cache
```

```python
import functools
import math

import jax
import jax.numpy as jnp
from jax import lax
from jax.experimental import pallas as pl
from jax.experimental.pallas import tpu as pltpu
from jax.sharding import PartitionSpec as P

MESH = pl.DeviceIdType.MESH
F32 = jnp.float32
BF16 = jnp.bfloat16

SIDE = 4
SEQ = SIDE * SIDE
HEADS = 8
DN = 128
DR = 64
DC = 512
DV = 128
WIDE = DC + 128
POS = 1024
SPAN = 64
ROWS = 16
COUNT = SPAN + ROWS
QROWS = HEADS * COUNT
SLICE = HEADS * (DN + DR)
TILE = 320
CHUNK = 256

SCALE2 = 0.1353 * math.log2(math.e)
LOW = -1e30


def dot(a, b):
    return jnp.dot(a, b, preferred_element_type=F32)


def dot_t(a, b):
    return lax.dot_general(a, b, (((1,), (1,)), ((), ())), preferred_element_type=F32)


def lane_mask(shape):
    return lax.broadcasted_iota(jnp.int32, shape, len(shape) - 1) < DR


def doubled(first):
    row = lax.broadcasted_iota(jnp.int32, (128, 128), 0)
    col = lax.broadcasted_iota(jnp.int32, (128, 128), 1)
    want = lax.rem(col, DR) + (0 if first else DR)
    return jnp.where(row == want, 1.0, 0.0).astype(BF16)


def kernel(
    q_ref, kv_ref, cache_ref, fill_ref, owner_ref, slot_ref, dlen_ref, uk_ref, uv_ref,
    span_ref, dec_ref, newc_ref,
    qbuf, kvbuf, q_all, qr_all, k_all, kr_all, k_own, acc, peak, total, score,
    o_send, e_send, o_recv, e_recv,
    local_sem, a_send, a_recv, c_send, c_recv, h_send, h_recv, p_send, p_recv,
):
    seq, grp = lax.axis_index("seq"), lax.axis_index("grp")
    core = lax.rem(grp, 2)
    z, x = seq // SIDE, lax.rem(seq, SIDE)

    def along_z(d):
        return lax.rem(z + d + SIDE, SIDE) * SIDE + x

    def along_x(d):
        return z * SIDE + lax.rem(x + d + SIDE, SIDE)

    def cache_peer(d):
        return (1 - core) * along_z(d) + core * along_x(d)

    def head_peer(d):
        return core * along_z(d) + (1 - core) * along_x(d)

    def remote(src, dst, send, recv, peer):
        return pltpu.make_async_remote_copy(
            src_ref=src, dst_ref=dst, send_sem=send, recv_sem=recv,
            device_id=(peer, grp), device_id_type=MESH,
        )

    barrier = pltpu.get_barrier_semaphore()
    for d in range(1, SEQ):
        pl.semaphore_signal(
            barrier, inc=1, device_id=(lax.rem(seq + d, SEQ), grp), device_id_type=MESH
        )

    own_q = pltpu.make_async_copy(
        q_ref.at[:, pl.ds(pl.multiple_of(seq * SLICE, 128), SLICE)], qbuf.at[seq], local_sem.at[0]
    )
    own_kv = pltpu.make_async_copy(kv_ref, kvbuf.at[seq], local_sem.at[1])
    own_q.start()
    own_kv.start()

    row = lax.broadcasted_iota(jnp.int32, (DR, 128), 0)
    col = lax.broadcasted_iota(jnp.int32, (DR, 128), 1)
    left = jnp.where(row == col, 1.0, 0.0).astype(BF16)
    right = jnp.where(row + DR == col, 1.0, 0.0).astype(BF16)
    rope_lo = cache_ref[0 : POS // 2, DC : DC + DR]
    rope_hi = cache_ref[POS // 2 : POS, DC : DC + DR]
    kr_all[0] = (dot(rope_lo, left) + dot(rope_hi, right)).astype(BF16)

    pl.semaphore_wait(barrier, SEQ - 1)

    exchange = []
    for d in range(1, SEQ):
        peer = lax.rem(seq + d, SEQ)
        exchange.append(
            remote(
                q_ref.at[:, pl.ds(pl.multiple_of(peer * SLICE, 128), SLICE)],
                qbuf.at[seq], a_send.at[d - 1], a_recv.at[d - 1], peer,
            )
        )
        exchange.append(
            remote(kv_ref, kvbuf.at[seq], a_send.at[SEQ + d - 2], a_recv.at[SEQ + d - 2], peer)
        )
    for c in exchange:
        c.start()

    def part(ref, slot, lo, n, width):
        return ref.at[slot, pl.ds(lo, n), pl.ds(0, width)]

    def ring(whole, packed, own, send, recv, peer_of, rows, packs):
        half, pack = rows // 2, packs // 2

        def pair(i, src_slot, dst_slot, h, peer):
            src = own.at[pl.ds(h * half, half), pl.ds(0, DC)]
            if src_slot:
                src = part(whole, src_slot, h * half, half, DC)
            return [
                remote(src, part(whole, dst_slot, h * half, half, DC), send.at[2 * i], recv.at[2 * i], peer),
                remote(
                    packed.at[src_slot, pl.ds(h * pack, pack)], packed.at[dst_slot, pl.ds(h * pack, pack)],
                    send.at[2 * i + 1], recv.at[2 * i + 1], peer,
                ),
            ]

        up, down = peer_of(1), peer_of(-1)
        first_up = pair(0, 0, 1, 0, up)
        first_down = pair(1, 0, 3, 1, down)
        second_up = pair(2, 0, 1, 1, up)
        second_down = pair(3, 0, 3, 0, down)
        onward_up = pair(4, 1, 2, 0, up)
        onward_down = pair(5, 3, 2, 1, down)
        return first_up, first_down, second_up, second_down, onward_up, onward_down

    def start(*groups):
        for g in groups:
            for c in g:
                c.start()

    def arrived(*groups):
        for g in groups:
            for c in g:
                c.wait_recv()

    def sent(*groups):
        for g in groups:
            for c in g:
                c.wait_send()

    cring = ring(k_all, kr_all, cache_ref, c_send, c_recv, cache_peer, POS, POS // 2)
    start(*cring[:4])

    lo2, hi2 = doubled(True), doubled(False)

    def unpack_keys(slot):
        k_all[slot, 0 : POS // 2, DC:WIDE] = dot(kr_all[slot], lo2).astype(BF16)
        k_all[slot, POS // 2 : POS, DC:WIDE] = dot(kr_all[slot], hi2).astype(BF16)

    def unpack_queries(slot):
        for p in range(HEADS // 2):
            both = qr_all[slot, COUNT * p : COUNT * (p + 1), :].astype(F32)
            mask = lane_mask(both.shape)
            at = 2 * COUNT * p
            q_all[slot, at : at + COUNT, DC:WIDE] = jnp.where(mask, both, 0.0).astype(BF16)
            q_all[slot, at + COUNT : at + 2 * COUNT, DC:WIDE] = jnp.where(mask, 0.0, both).astype(BF16)

    k_all[0, :, 0:DC] = cache_ref[:, 0:DC]
    unpack_keys(0)
    peak[...] = jnp.full(peak.shape, LOW, F32)
    total[...] = jnp.zeros(total.shape, F32)
    acc[...] = jnp.zeros(acc.shape, F32)

    own_q.wait()
    own_kv.wait()
    for c in exchange:
        c.wait_recv()
    prow = lax.broadcasted_iota(jnp.int32, (COUNT, 128), 0)
    pcol = lax.broadcasted_iota(jnp.int32, (COUNT, 128), 1)
    place = jnp.where(prow < SPAN, 8 * (prow // 4) + lax.rem(prow, 4), 8 * (prow - SPAN) + 4)
    order = jnp.where(pcol == place, 1.0, 0.0).astype(BF16)
    q_rows = qbuf[...].astype(F32).reshape(8 * SEQ, SLICE).astype(BF16)
    q_rows = dot(order, q_rows)
    for p in range(HEADS // 2):
        at = 3 * 128 * p
        t0, t1, t2 = (q_rows[:, at + 128 * i : at + 128 * (i + 1)] for i in range(3))
        mask = lane_mask(t0.shape)
        nope = t0.astype(BF16)
        swapped = jnp.where(mask, t2, t1).astype(BF16)
        qr_all[0, COUNT * p : COUNT * (p + 1), :] = jnp.where(mask, t1, t2).astype(BF16)
        weight = uk_ref[2 * p + 1]
        weight = jnp.concatenate([weight[DR:], weight[:DR]], axis=0)
        row0 = 2 * COUNT * p
        q_all[0, row0 : row0 + COUNT, 0:DC] = dot(nope, uk_ref[2 * p]).astype(BF16)
        q_all[0, row0 + COUNT : row0 + 2 * COUNT, 0:DC] = dot(swapped, weight).astype(BF16)

    hring = ring(q_all, qr_all, q_all.at[0], h_send, h_recv, head_peer, QROWS, QROWS // 2)
    start(*hring[:4])
    unpack_queries(0)

    kv_rows = kvbuf[...].astype(F32).reshape(8 * SEQ, WIDE).astype(BF16)
    kv_rows = dot(order, kv_rows).astype(BF16)
    k_own[...] = jnp.zeros(k_own.shape, BF16)
    k_own[0:COUNT, 0:DC] = kv_rows[:, 0:DC]
    k_own[0:COUNT, DC:WIDE] = dot(kv_rows[:, DC:WIDE], lo2).astype(BF16)

    target = jnp.where(owner_ref[...] == seq, slot_ref[...], -1)
    span_rows = kv_rows[0:SPAN, 0 : DC + DR]

    @pl.loop(0, POS // 128)
    def _(i):
        at = pl.multiple_of(i * 128, 128)
        local = lax.broadcasted_iota(jnp.int32, (128, SPAN), 0) + at
        hot = jnp.where(local == target, 1.0, 0.0)
        put = dot(hot.astype(BF16), span_rows)
        any_hot = jnp.sum(hot, axis=1, keepdims=True) > 0.0
        old = cache_ref[pl.ds(at, 128), :].astype(F32)
        newc_ref[pl.ds(at, 128), :] = jnp.where(any_hot, put, old).astype(BF16)

    def attend(hs, ks):
        fill = fill_ref[cache_peer_back(ks)]

        @pl.loop(0, QROWS // TILE)
        def _(t):
            rows = pl.ds(pl.multiple_of(t * TILE, TILE), TILE)
            queries = q_all[hs, rows, :]
            top = peak[hs, rows, :]
            old = top
            for j in range(POS // CHUNK):
                s = dot_t(queries, k_all[ks, j * CHUNK : (j + 1) * CHUNK, :])
                at = lax.broadcasted_iota(jnp.int32, (1, CHUNK), 1) + j * CHUNK
                s = jnp.where(at < fill, s, LOW)
                score[:, j * CHUNK : (j + 1) * CHUNK] = s
                top = jnp.maximum(top, jnp.max(s, axis=1, keepdims=True))
            keep = jnp.exp2((old - top) * SCALE2)
            out = jnp.zeros((TILE, DC), F32)
            add = jnp.zeros((TILE, 1), F32)
            for j in range(POS // CHUNK):
                e = jnp.exp2((score[:, j * CHUNK : (j + 1) * CHUNK] - top) * SCALE2)
                add += jnp.sum(e, axis=1, keepdims=True)
                out += dot(e.astype(BF16), k_all[ks, j * CHUNK : (j + 1) * CHUNK, 0:DC])
            peak[hs, rows, :] = top
            total[hs, rows, :] = total[hs, rows, :] * keep + add
            acc[hs, rows, :] = acc[hs, rows, :] * keep + out

    def cache_peer_back(ks):
        return cache_peer(-ks)

    eye = lax.broadcasted_iota(jnp.int32, (128, 128), 0) == lax.broadcasted_iota(
        jnp.int32, (128, 128), 1
    )

    def finish(hs):
        t = total[hs]
        o_send[hs - 1] = (acc[hs] * (1.0 / t)).astype(BF16)
        level = peak[hs] * SCALE2 + jnp.log2(t)
        for i in range(QROWS // 128):
            square = jnp.broadcast_to(level[128 * i : 128 * (i + 1)], (128, 128))
            e_send[hs - 1, i : i + 1, :] = jnp.sum(jnp.where(eye, square, 0.0), axis=0, keepdims=True)

    def back(hs):
        peer = head_peer(-hs)
        return [
            remote(o_send.at[hs - 1], o_recv.at[hs - 1], p_send.at[2 * hs - 2], p_recv.at[2 * hs - 2], peer),
            remote(e_send.at[hs - 1], e_recv.at[hs - 1], p_send.at[2 * hs - 1], p_recv.at[2 * hs - 1], peer),
        ]

    e_send[...] = jnp.zeros(e_send.shape, F32)
    attend(0, 0)

    qrow = lax.broadcasted_iota(jnp.int32, (COUNT, 128), 0)
    kcol = lax.broadcasted_iota(jnp.int32, (COUNT, 128), 1)
    limit = jnp.where(qrow < SPAN, qrow + 1, 0)
    for r in range(ROWS):
        limit = jnp.where(qrow == SPAN + r, dlen_ref[r], limit)
    seen = (kcol < limit) | ((qrow >= SPAN) & (kcol == qrow))
    for h in range(HEADS):
        rows = slice(COUNT * h, COUNT * (h + 1))
        s = jnp.where(seen, dot_t(q_all[0, rows, :], k_own[...]), LOW)
        old = peak[0, rows, :]
        top = jnp.maximum(old, jnp.max(s, axis=1, keepdims=True))
        keep = jnp.exp2((old - top) * SCALE2)
        e = jnp.exp2((s - top) * SCALE2)
        peak[0, rows, :] = top
        total[0, rows, :] = total[0, rows, :] * keep + jnp.sum(e, axis=1, keepdims=True)
        acc[0, rows, :] = acc[0, rows, :] * keep + dot(e.astype(BF16), k_own[:, 0:DC])

    arrived(hring[0], hring[1])
    start(hring[4], hring[5])
    arrived(hring[2], hring[3])
    unpack_queries(1)
    unpack_queries(3)

    @pl.loop(0, 2)
    def _(i):
        attend(1 + 2 * i, 0)

    arrived(cring[0], cring[1])
    start(cring[4], cring[5])
    arrived(cring[2], cring[3])
    unpack_keys(1)
    unpack_keys(3)

    @pl.loop(0, 6)
    def _(i):
        j = lax.rem(i, 3)
        attend(j + j // 2, 1 + 2 * (i // 3))

    arrived(hring[4], hring[5])
    unpack_queries(2)

    @pl.loop(0, 3)
    def _(i):
        attend(2, i + i // 2)

    arrived(cring[4], cring[5])
    unpack_keys(2)

    @pl.loop(0, 3)
    def _(i):
        hs = 2 - i + 3 * (i // 2)
        attend(hs, 2)
        finish(hs)
        start(back(hs))

    attend(0, 2)

    own_level = peak[0] * SCALE2 + jnp.log2(total[0])
    levels = []
    for hs in range(1, SIDE):
        arrived(back(hs))
        column = []
        for i in range(QROWS // 128):
            square = jnp.broadcast_to(e_recv[hs - 1, i : i + 1, :], (128, 128))
            column.append(jnp.sum(jnp.where(eye, square, 0.0), axis=1, keepdims=True))
        levels.append(jnp.concatenate(column, axis=0))
    top = own_level
    for level in levels:
        top = jnp.maximum(top, level)
    weight = jnp.exp2(own_level - top)
    norm = weight
    shares = []
    for level in levels:
        share = jnp.exp2(level - top)
        shares.append(share)
        norm = norm + share
    norm = 1.0 / norm
    first = weight * norm / total[0]
    shares = [share * norm for share in shares]
    for h in range(HEADS):
        rows = slice(COUNT * h, COUNT * (h + 1))
        latent = acc[0, rows, :] * first[rows]
        for i in range(SIDE - 1):
            latent = latent + o_recv[i, rows, :].astype(F32) * shares[i][rows]
        value = dot(latent.astype(BF16), uv_ref[h]).astype(BF16)
        span_ref[:, DV * h : DV * (h + 1)] = value[0:SPAN]
        dec_ref[:, DV * h : DV * (h + 1)] = value[SPAN:COUNT]

    for c in exchange:
        c.wait_send()
    sent(*cring, *hring)
    for hs in range(1, SIDE):
        sent(back(hs))


def body(query, dec_query, cache_kv, span_kv, dec_kv, cache_fill, owner, slot, dec_len, w_uk, w_uv):
    fours = query.shape[0]
    q = jnp.concatenate(
        [query, dec_query, jnp.zeros((8 - fours - 1, query.shape[1]), query.dtype)], axis=0
    )
    kv = jnp.concatenate([span_kv, dec_kv], axis=0)
    kv = jnp.pad(kv, ((0, 8 - kv.shape[0]), (0, WIDE - kv.shape[1])))
    vmem = pl.BlockSpec(memory_space=pltpu.VMEM)
    smem = pl.BlockSpec(memory_space=pltpu.SMEM)
    dma = pltpu.SemaphoreType.DMA
    return pl.pallas_call(
        kernel,
        out_shape=(
            jax.ShapeDtypeStruct((SPAN, HEADS * DV), BF16),
            jax.ShapeDtypeStruct((ROWS, HEADS * DV), BF16),
            jax.ShapeDtypeStruct((POS, DC + DR), BF16),
        ),
        in_specs=[vmem, vmem, vmem, smem, vmem, vmem, smem, vmem, vmem],
        out_specs=(vmem, vmem, vmem),
        scratch_shapes=[
            pltpu.VMEM((SEQ, 8, SLICE), BF16),
            pltpu.VMEM((SEQ, 8, WIDE), BF16),
            pltpu.VMEM((SIDE, QROWS, WIDE), BF16),
            pltpu.VMEM((SIDE, QROWS // 2, 128), BF16),
            pltpu.VMEM((SIDE, POS, WIDE), BF16),
            pltpu.VMEM((SIDE, POS // 2, 128), BF16),
            pltpu.VMEM((128, WIDE), BF16),
            pltpu.VMEM((SIDE, QROWS, DC), F32),
            pltpu.VMEM((SIDE, QROWS, 1), F32),
            pltpu.VMEM((SIDE, QROWS, 1), F32),
            pltpu.VMEM((TILE, POS), F32),
            pltpu.VMEM((SIDE - 1, QROWS, DC), BF16),
            pltpu.VMEM((SIDE - 1, 8, 128), F32),
            pltpu.VMEM((SIDE - 1, QROWS, DC), BF16),
            pltpu.VMEM((SIDE - 1, 8, 128), F32),
            dma((2,)),
            dma((2 * (SEQ - 1),)),
            dma((2 * (SEQ - 1),)),
            dma((12,)),
            dma((12,)),
            dma((12,)),
            dma((12,)),
            dma((6,)),
            dma((6,)),
        ],
        compiler_params=pltpu.CompilerParams(
            collective_id=0, has_side_effects=True, vmem_limit_bytes=56 * 2**20
        ),
        cost_estimate=pl.CostEstimate(
            flops=2 * SIDE * SIDE * QROWS * POS * (DC + DR + DC),
            bytes_accessed=8 * 2**20,
            transcendentals=SIDE * SIDE * QROWS * POS,
        ),
    )(
        q, kv, cache_kv, cache_fill, owner.reshape(1, SPAN), slot.reshape(1, SPAN), dec_len, w_uk, w_uv,
    )


def solution(mesh):
    in_specs = (
        P(("grp", "seq"), None),
        P(("grp", "seq"), None),
        P(("grp", "seq"), None),
        P(("grp", "seq"), None),
        P(("grp", "seq"), None),
        P("grp"),
        P("grp"),
        P("grp"),
        P("grp"),
        P("seq", None, None),
        P("seq", None, None),
    )
    out_specs = (P("grp", "seq"), P("grp", "seq"), P(("grp", "seq"), None))
    return jax.shard_map(body, mesh=mesh, in_specs=in_specs, out_specs=out_specs, check_vma=False)
```

```python
import functools
import math

import jax
import jax.numpy as jnp
from jax import lax
from jax.experimental import pallas as pl
from jax.experimental.pallas import tpu as pltpu
from jax.sharding import PartitionSpec as P

MESH = pl.DeviceIdType.MESH
F32 = jnp.float32
BF16 = jnp.bfloat16

SIDE = 4
SEQ = SIDE * SIDE
HEADS = 8
DN = 128
DR = 64
DC = 512
DV = 128
KEY = DC + DR
WIDE = DC + 128
POS = 1024
SPAN = 64
ROWS = 16
COUNT = SPAN + ROWS
BAND = HEADS // 2 * COUNT
SLICE = HEADS * (DN + DR)
MESSAGE = SLICE + WIDE
CHUNK = 256

SCALE2 = 0.1353 * math.log2(math.e)
LOW = -1e30

ORDER_BAND = (0, 1, 2, 7, 3, 6, 4, 5) + (4, 5, 2, 3, 6, 7) * 3 + (0, 1, 0, 1, 0, 1)
ORDER_KEYS = (0,) * 8 + (1,) * 6 + (3,) * 6 + (2,) * 6 + (1, 1, 3, 3, 2, 2)
STEPS = len(ORDER_BAND)
FINISH = 20


def dot(a, b):
    return jnp.dot(a, b, preferred_element_type=F32)


def dot_t(a, b):
    return lax.dot_general(a, b, (((1,), (1,)), ((), ())), preferred_element_type=F32)


def lane_mask(shape):
    return lax.broadcasted_iota(jnp.int32, shape, len(shape) - 1) < DR


def doubled():
    row = lax.broadcasted_iota(jnp.int32, (128, 128), 0)
    col = lax.broadcasted_iota(jnp.int32, (128, 128), 1)
    return jnp.where(row == lax.rem(col, DR), 1.0, 0.0).astype(BF16)


def pick(table, i):
    value = 0
    for at, entry in enumerate(table):
        if entry:
            value = value + entry * jnp.where(i == at, 1, 0)
    return value


def kernel(
    query_ref, dec_query_ref, span_kv_ref, dec_kv_ref, cache_ref, fill_ref, owner_ref, slot_ref, dlen_ref,
    uk_hbm, uv_hbm,
    out_ref, newc_hbm,
    rows8, kv8, a_out, a_in, q_all, qr_all, k_all, k_own, uk, uv, newc,
    acc, peak, total, score_a, score_b, best_a, best_b, weights, o_send, e_send, o_recv, e_recv,
    local_sem, a_send, a_recv, c_send, c_recv, h_send, h_recv, p_send, p_recv,
):
    seq, grp = lax.axis_index("seq"), lax.axis_index("grp")
    core = lax.rem(grp, 2)
    z, x = seq // SIDE, lax.rem(seq, SIDE)

    def along_z(d):
        return lax.rem(z + d + SIDE, SIDE) * SIDE + x

    def along_x(d):
        return z * SIDE + lax.rem(x + d + SIDE, SIDE)

    def cache_peer(d):
        return (1 - core) * along_z(d) + core * along_x(d)

    def head_peer(d):
        return core * along_z(d) + (1 - core) * along_x(d)

    def remote(src, dst, send, recv, peer):
        return pltpu.make_async_remote_copy(
            src_ref=src, dst_ref=dst, send_sem=send, recv_sem=recv,
            device_id=(peer, grp), device_id_type=MESH,
        )

    barrier = pltpu.get_barrier_semaphore()
    for d in range(1, SEQ):
        pl.semaphore_signal(
            barrier, inc=1, device_id=(lax.rem(seq + d, SEQ), grp), device_id_type=MESH
        )

    own_keys = pltpu.make_async_copy(cache_ref, k_all.at[0, pl.ds(0, KEY)], local_sem.at[0])
    own_uk = pltpu.make_async_copy(uk_hbm, uk, local_sem.at[1])
    own_uv = pltpu.make_async_copy(uv_hbm, uv, local_sem.at[2])
    own_keys.start()
    own_uk.start()
    own_uv.start()

    rows8[...] = jnp.zeros(rows8.shape, F32)
    rows8[0:4, :] = query_ref[...].astype(F32)
    rows8[4:5, :] = dec_query_ref[...].astype(F32)
    kv8[...] = jnp.zeros(kv8.shape, F32)
    kv8[0:4, 0:KEY] = span_kv_ref[...].astype(F32)
    kv8[4:5, 0:KEY] = dec_kv_ref[...].astype(F32)
    kv = kv8[...].astype(BF16)
    for s in range(SEQ):
        a_out[s, :, 0:SLICE] = rows8[:, s * SLICE : (s + 1) * SLICE].astype(BF16)
        a_out[s, :, SLICE:MESSAGE] = kv
    a_in[seq] = a_out[seq]

    pl.semaphore_wait(barrier, SEQ - 1)

    exchange = []
    for d in range(1, SEQ):
        peer = lax.rem(seq + d, SEQ)
        exchange.append(remote(a_out.at[peer], a_in.at[seq], a_send.at[d - 1], a_recv.at[d - 1], peer))
    for c in exchange:
        c.start()

    def ring(halves, send, recv, peer_of):
        count = len(halves(0, 0))

        def pair(i, src_slot, dst_slot, h, peer):
            src, dst = halves(src_slot, h), halves(dst_slot, h)
            return [
                remote(src[k], dst[k], send.at[count * i + k], recv.at[count * i + k], peer)
                for k in range(count)
            ]

        up, down = peer_of(1), peer_of(-1)
        first_up = pair(0, 0, 1, 0, up)
        first_down = pair(1, 0, 3, 1, down)
        second_up = pair(2, 0, 1, 1, up)
        second_down = pair(3, 0, 3, 0, down)
        onward_up = pair(4, 1, 2, 0, up)
        onward_down = pair(5, 3, 2, 1, down)
        return first_up, first_down, second_up, second_down, onward_up, onward_down

    def key_half(slot, h):
        return [k_all.at[slot, pl.ds(0, KEY), pl.ds(h * (POS // 2), POS // 2)]]

    def query_half(slot, h):
        return [q_all.at[2 * slot + h, pl.ds(0, BAND), pl.ds(0, DC)], qr_all.at[2 * slot + h]]

    def start(*groups):
        for g in groups:
            for c in g:
                c.start()

    def arrived(*groups):
        for g in groups:
            for c in g:
                c.wait_recv()

    def sent(*groups):
        for g in groups:
            for c in g:
                c.wait_send()

    cring = ring(key_half, c_send, c_recv, cache_peer)
    hring = ring(query_half, h_send, h_recv, head_peer)

    def unpack_keys(slot):
        k_all[slot, KEY:WIDE, :] = k_all[slot, DC:KEY, :]

    def unpack_queries(band):
        for p in range(HEADS // 4):
            both = qr_all[band, COUNT * p : COUNT * (p + 1), :].astype(F32)
            mask = lane_mask(both.shape)
            at = 2 * COUNT * p
            q_all[band, at : at + COUNT, DC:WIDE] = jnp.where(mask, both, 0.0).astype(BF16)
            q_all[band, at + COUNT : at + 2 * COUNT, DC:WIDE] = jnp.where(mask, 0.0, both).astype(BF16)

    own_keys.wait()
    start(cring[0], cring[1])
    unpack_keys(0)
    peak[...] = jnp.full(peak.shape, LOW, F32)
    total[...] = jnp.zeros(total.shape, F32)
    acc[...] = jnp.zeros(acc.shape, F32)
    e_send[...] = jnp.zeros(e_send.shape, F32)

    prow = lax.broadcasted_iota(jnp.int32, (COUNT, 128), 0)
    pcol = lax.broadcasted_iota(jnp.int32, (COUNT, 128), 1)
    place = jnp.where(prow < SPAN, 8 * (prow // 4) + lax.rem(prow, 4), 8 * (prow - SPAN) + 4)
    order = jnp.where(pcol == place, 1.0, 0.0).astype(BF16)
    own_uk.wait()
    for c in exchange:
        c.wait_recv()
    got = a_in[...].astype(F32).reshape(8 * SEQ, MESSAGE).astype(BF16)
    got = dot(order, got)
    for p in range(HEADS // 2):
        at = 3 * 128 * p
        t0, t1, t2 = (got[:, at + 128 * i : at + 128 * (i + 1)] for i in range(3))
        mask = lane_mask(t0.shape)
        nope = t0.astype(BF16)
        swapped = jnp.where(mask, t2, t1).astype(BF16)
        band, pair = p // 2, p % 2
        qr_all[band, COUNT * pair : COUNT * (pair + 1), :] = jnp.where(mask, t1, t2).astype(BF16)
        weight = uk[2 * p + 1]
        weight = jnp.concatenate([weight[DR:], weight[:DR]], axis=0)
        row0 = 2 * COUNT * pair
        q_all[band, row0 : row0 + COUNT, 0:DC] = dot(nope, uk[2 * p]).astype(BF16)
        q_all[band, row0 + COUNT : row0 + 2 * COUNT, 0:DC] = dot(swapped, weight).astype(BF16)
        if p == 1:
            start(hring[0])
        if p == 3:
            start(hring[1], hring[2], hring[3])
    unpack_queries(0)
    unpack_queries(1)

    kv_rows = got[:, SLICE:MESSAGE].astype(BF16)
    k_own[...] = jnp.zeros(k_own.shape, BF16)
    k_own[0:COUNT, 0:DC] = kv_rows[:, 0:DC]
    k_own[0:COUNT, DC:WIDE] = dot(kv_rows[:, DC:WIDE], doubled()).astype(BF16)

    def scores(band, ks, out, best):
        fill = fill_ref[cache_peer(-ks)]
        top = None
        for j in range(POS // CHUNK):
            at = slice(j * CHUNK, (j + 1) * CHUNK)
            s = dot(q_all[band], k_all[ks, :, at])
            local = lax.broadcasted_iota(jnp.int32, (1, CHUNK), 1) + j * CHUNK
            s = jnp.where(local < fill, s, LOW)
            out[:, at] = s
            for u in range(0, CHUNK, 128):
                top = s[:, u : u + 128] if top is None else jnp.maximum(top, s[:, u : u + 128])
            yield
        best[...] = top

    def attend(band, ks, now, later, ahead):
        score, best = now
        old = peak[band]
        top = jnp.maximum(old, jnp.max(best[...], axis=1, keepdims=True))
        keep = jnp.exp2((old - top) * SCALE2)
        add = None
        nxt = scores(*ahead, *later)
        for j in range(POS // CHUNK):
            next(nxt)
            at = slice(j * CHUNK, (j + 1) * CHUNK)
            e = jnp.exp2((score[:, at] - top) * SCALE2)
            weights[:, at] = e.astype(BF16)
            for u in range(0, CHUNK, 128):
                add = e[:, u : u + 128] if add is None else add + e[:, u : u + 128]
        next(nxt, None)
        out = dot_t(weights[...], k_all[ks, 0:DC, :])
        peak[band] = top
        total[band] = total[band] * keep + jnp.sum(add, axis=1, keepdims=True)
        acc[band] = acc[band] * keep + out

    eye = lax.broadcasted_iota(jnp.int32, (64, 128), 0) == lax.broadcasted_iota(jnp.int32, (64, 128), 1)

    def finish(band):
        t = total[band]
        o_send[band - 2] = (acc[band] * (1.0 / t)).astype(BF16)
        level = peak[band] * SCALE2 + jnp.log2(t)
        for i in range(BAND // 64):
            square = jnp.broadcast_to(level[64 * i : 64 * (i + 1)], (64, 128))
            e_send[band - 2, i : i + 1, :] = jnp.sum(jnp.where(eye, square, 0.0), axis=0, keepdims=True)

    def back(band):
        peer, i = head_peer(-(band // 2)), band - 2
        return [
            remote(o_send.at[i], o_recv.at[i], p_send.at[2 * i], p_recv.at[2 * i], peer),
            remote(e_send.at[i], e_recv.at[i], p_send.at[2 * i + 1], p_recv.at[2 * i + 1], peer),
        ]

    qrow = lax.broadcasted_iota(jnp.int32, (COUNT, 128), 0)
    kcol = lax.broadcasted_iota(jnp.int32, (COUNT, 128), 1)
    limit = jnp.where(qrow < SPAN, qrow + 1, 0)
    for r in range(ROWS):
        limit = jnp.where(qrow == SPAN + r, dlen_ref[r], limit)
    seen = (kcol < limit) | ((qrow >= SPAN) & (kcol == qrow))
    hidden = jnp.where(seen, 0.0, 1.0)
    hidden = jnp.concatenate([hidden] * (HEADS // 2), axis=0)
    for band in range(2):
        s = jnp.where(hidden > 0.5, LOW, dot_t(q_all[band], k_own[...]))
        top = jnp.max(s, axis=1, keepdims=True)
        e = jnp.exp2((s - top) * SCALE2)
        peak[band] = top
        total[band] = jnp.sum(e, axis=1, keepdims=True)
        acc[band] = dot(e.astype(BF16), k_own[:, 0:DC])

    target = jnp.where(owner_ref[...] == seq, slot_ref[...], -1)
    span_rows = kv_rows[0:SPAN, 0:KEY]

    @pl.loop(0, POS // 256)
    def _(i):
        at = pl.ds(pl.multiple_of(i * 256, 256), 256)
        local = lax.broadcasted_iota(jnp.int32, (256, SPAN), 0) + i * 256
        hot = jnp.where(local == target, 1.0, 0.0).astype(BF16)
        put = lax.dot_general(span_rows, hot, (((0,), (1,)), ((), ())), preferred_element_type=F32)
        any_hot = dot_t(jnp.ones((8, SPAN), BF16), hot)[0:1] > 0.5
        old = k_all[0, 0:KEY, at].astype(F32)
        newc[:, at] = jnp.where(any_hot, put, old).astype(BF16)

    put_cache = pltpu.make_async_copy(newc, newc_hbm, local_sem.at[3])
    put_cache.start()

    def before(i):
        @pl.when(i == 1)
        def _():
            arrived(hring[0], hring[1])
            start(hring[4], hring[5])
            start(cring[2], cring[3])
            unpack_queries(2)
            unpack_queries(7)

        @pl.when(i == 3)
        def _():
            arrived(hring[2], hring[3])
            unpack_queries(3)
            unpack_queries(6)
            arrived(cring[0], cring[1])
            start(cring[4], cring[5])

        @pl.when(i == 5)
        def _():
            arrived(hring[4], hring[5])
            unpack_queries(4)
            unpack_queries(5)

        @pl.when(i == 7)
        def _():
            arrived(cring[2])
            unpack_keys(1)

        @pl.when(i == 13)
        def _():
            arrived(cring[3])
            unpack_keys(3)

        @pl.when(i == 19)
        def _():
            arrived(cring[4], cring[5])
            unpack_keys(2)

    def after(i, band):
        @pl.when((i >= FINISH) & (i < FINISH + 6))
        def _():
            finish(band)
            start(back(band))

    a, b = (score_a, best_a), (score_b, best_b)
    for _ in scores(0, 0, *a):
        pass

    def step(i, now, later):
        before(i)
        band, ks = pick(ORDER_BAND, i), pick(ORDER_KEYS, i)
        ahead = jnp.minimum(i + 1, STEPS - 1)
        attend(band, ks, now, later, (pick(ORDER_BAND, ahead), pick(ORDER_KEYS, ahead)))
        after(i, band)

    @pl.loop(0, STEPS // 2)
    def _(i):
        step(2 * i, a, b)
        step(2 * i + 1, b, a)

    own_uv.wait()
    for half in range(2):
        levels = []
        for s in range(1, SIDE):
            i = 2 * s + half - 2
            arrived(back(i + 2))
            column = []
            for j in range(BAND // 64):
                square = jnp.broadcast_to(e_recv[i, j : j + 1, :], (64, 128))
                column.append(jnp.sum(jnp.where(eye, square, 0.0), axis=1, keepdims=True))
            levels.append(jnp.concatenate(column, axis=0))
        own_level = peak[half] * SCALE2 + jnp.log2(total[half])
        top = own_level
        for level in levels:
            top = jnp.maximum(top, level)
        weight = jnp.exp2(own_level - top)
        shares = [jnp.exp2(level - top) for level in levels]
        norm = 1.0 / (weight + shares[0] + shares[1] + shares[2])
        first = weight * norm / total[half]
        shares = [share * norm for share in shares]
        for h in range(HEADS // 2):
            rows = slice(COUNT * h, COUNT * (h + 1))
            latent = acc[half, rows, :] * first[rows]
            for s in range(SIDE - 1):
                latent = latent + o_recv[2 * s + half, rows, :].astype(F32) * shares[s][rows]
            head = HEADS // 2 * half + h
            value = dot(latent.astype(BF16), uv[head])
            out_ref[:, DV * head : DV * (head + 1)] = value.astype(BF16)

    put_cache.wait()
    for c in exchange:
        c.wait_send()
    sent(*cring, *hring)
    for band in range(2, 2 * SIDE):
        sent(back(band))


def hand_over(out_ref, cache_ref, span_ref, dec_ref, new_ref, out, cache, sem):
    half = KEY // 2
    ins = [pltpu.make_async_copy(out_ref, out, sem.at[0])]
    outs = [
        [
            pltpu.make_async_copy(out.at[pl.ds(0, SPAN)], span_ref, sem.at[3]),
            pltpu.make_async_copy(out.at[pl.ds(SPAN, ROWS)], dec_ref, sem.at[4]),
        ]
    ]
    for i in range(2):
        rows = pl.ds(i * half, half)
        ins.append(pltpu.make_async_copy(cache_ref.at[rows], cache.at[rows], sem.at[1 + i]))
        outs.append([pltpu.make_async_copy(cache.at[rows], new_ref.at[rows], sem.at[5 + i])])
    for c in ins:
        c.start()
    for c, then in zip(ins, outs):
        c.wait()
        for d in then:
            d.start()
    for then in outs:
        for d in then:
            d.wait()


def body(query, dec_query, cache_kv, span_kv, dec_kv, cache_fill, owner, slot, dec_len, w_uk, w_uv):
    vmem = pl.BlockSpec(memory_space=pltpu.VMEM)
    smem = pl.BlockSpec(memory_space=pltpu.SMEM)
    hbm = pl.BlockSpec(memory_space=pl.ANY)
    dma = pltpu.SemaphoreType.DMA
    shape = jax.ShapeDtypeStruct
    out, new_cache = pl.pallas_call(
        kernel,
        out_shape=(shape((COUNT, HEADS * DV), BF16), shape((KEY, POS), BF16)),
        in_specs=[vmem, vmem, vmem, vmem, hbm, smem, vmem, vmem, smem, hbm, hbm],
        out_specs=(vmem, hbm),
        scratch_shapes=[
            pltpu.VMEM((8, SEQ * SLICE), F32),
            pltpu.VMEM((8, WIDE), F32),
            pltpu.VMEM((SEQ, 8, MESSAGE), BF16),
            pltpu.VMEM((SEQ, 8, MESSAGE), BF16),
            pltpu.VMEM((2 * SIDE, BAND, WIDE), BF16),
            pltpu.VMEM((2 * SIDE, BAND // 2, 128), BF16),
            pltpu.VMEM((SIDE, WIDE, POS), BF16),
            pltpu.VMEM((128, WIDE), BF16),
            pltpu.VMEM((HEADS, DN, DC), BF16),
            pltpu.VMEM((HEADS, DC, DV), BF16),
            pltpu.VMEM((KEY, POS), BF16),
            pltpu.VMEM((2 * SIDE, BAND, DC), F32),
            pltpu.VMEM((2 * SIDE, BAND, 1), F32),
            pltpu.VMEM((2 * SIDE, BAND, 1), F32),
            pltpu.VMEM((BAND, POS), F32),
            pltpu.VMEM((BAND, POS), F32),
            pltpu.VMEM((BAND, 128), F32),
            pltpu.VMEM((BAND, 128), F32),
            pltpu.VMEM((BAND, POS), BF16),
            pltpu.VMEM((6, BAND, DC), BF16),
            pltpu.VMEM((6, 8, 128), F32),
            pltpu.VMEM((6, BAND, DC), BF16),
            pltpu.VMEM((6, 8, 128), F32),
            dma((4,)),
            dma((SEQ - 1,)),
            dma((SEQ - 1,)),
            dma((6,)),
            dma((6,)),
            dma((12,)),
            dma((12,)),
            dma((12,)),
            dma((12,)),
        ],
        compiler_params=pltpu.CompilerParams(
            collective_id=0, has_side_effects=True, vmem_limit_bytes=56 * 2**20
        ),
        cost_estimate=pl.CostEstimate(
            flops=2 * STEPS * BAND * POS * (KEY + DC),
            bytes_accessed=8 * 2**20,
            transcendentals=STEPS * BAND * POS,
        ),
    )(
        query, dec_query, span_kv, dec_kv, cache_kv.T, cache_fill,
        owner.reshape(1, SPAN), slot.reshape(1, SPAN), dec_len, w_uk, w_uv,
    )
    span_out, dec_out, new_cache = pl.pallas_call(
        hand_over,
        out_shape=(
            shape((SPAN, HEADS * DV), BF16),
            shape((ROWS, HEADS * DV), BF16),
            shape((KEY, POS), BF16),
        ),
        in_specs=[hbm, hbm],
        out_specs=(hbm, hbm, hbm),
        scratch_shapes=[
            pltpu.VMEM((COUNT, HEADS * DV), BF16),
            pltpu.VMEM((KEY, POS), BF16),
            dma((7,)),
        ],
        compiler_params=pltpu.CompilerParams(vmem_limit_bytes=60 * 2**20),
        cost_estimate=pl.CostEstimate(flops=0, bytes_accessed=3 * 2**20, transcendentals=0),
    )(out, new_cache)
    return span_out, dec_out, new_cache.T


def solution(mesh):
    in_specs = (
        P(("grp", "seq"), None),
        P(("grp", "seq"), None),
        P(("grp", "seq"), None),
        P(("grp", "seq"), None),
        P(("grp", "seq"), None),
        P("grp"),
        P("grp"),
        P("grp"),
        P("grp"),
        P("seq", None, None),
        P("seq", None, None),
    )
    out_specs = (P("grp", "seq"), P("grp", "seq"), P(("grp", "seq"), None))
    return jax.shard_map(body, mesh=mesh, in_specs=in_specs, out_specs=out_specs, check_vma=False)
```

```python
import functools
import math

import jax
import jax.numpy as jnp
from jax import lax
from jax.experimental import pallas as pl
from jax.experimental.pallas import tpu as pltpu
from jax.sharding import PartitionSpec as P

MESH = pl.DeviceIdType.MESH
F32 = jnp.float32
BF16 = jnp.bfloat16

SIDE = 4
SEQ = SIDE * SIDE
HEADS = 8
DN = 128
DR = 64
DC = 512
DV = 128
KEY = DC + DR
WIDE = DC + 128
POS = 1024
SPAN = 64
ROWS = 16
COUNT = SPAN + ROWS
BAND = HEADS // 2 * COUNT
SLICE = HEADS * (DN + DR)
CHUNK = 256

SCALE2 = 0.1353 * math.log2(math.e)
LOW = -1e30

PIECES = ((0, 0), (0, 1), (1, 0), (3, 1), (1, 1), (3, 0), (2, 0), (2, 1))
HALF = POS // 2
ORDER_BAND = (0, 1, 2, 7, 3, 6, 4, 5) + (4, 5, 2, 3, 6, 7) * 3 + (0, 1, 0, 1, 0, 1)
ORDER_KEYS = (0,) * 8 + (1,) * 6 + (2,) * 6 + (3,) * 6 + (1, 1, 2, 2, 3, 3)
STEPS = len(ORDER_BAND)
FINISH = 20


def dot(a, b):
    return jnp.dot(a, b, preferred_element_type=F32)


def dot_t(a, b):
    return lax.dot_general(a, b, (((1,), (1,)), ((), ())), preferred_element_type=F32)


def lane_mask(shape):
    return lax.broadcasted_iota(jnp.int32, shape, len(shape) - 1) < DR


def doubled():
    row = lax.broadcasted_iota(jnp.int32, (128, 128), 0)
    col = lax.broadcasted_iota(jnp.int32, (128, 128), 1)
    return jnp.where(row == lax.rem(col, DR), 1.0, 0.0).astype(BF16)


def pick(table, i):
    word = None
    for lo in reversed(range(0, len(table), 8)):
        packed = sum(entry << (4 * at) for at, entry in enumerate(table[lo : lo + 8]))
        word = jnp.int32(packed) if word is None else jnp.where(i < lo + 8, jnp.int32(packed), word)
    return lax.shift_right_logical(word, 4 * lax.rem(i, 8)) & 7


def kernel(
    query_ref, dec_query_ref, span_kv_ref, dec_kv_ref, cache_ref, fill_ref, owner_ref, slot_ref, dlen_ref,
    uk_hbm, uv_hbm,
    out_ref, newc_hbm,
    rows8, kv8, a_out, a_in, kv_out, kv_in, q_all, qr_all, k_all, k_own, uk, uv, newc,
    acc, peak, total, score_a, score_b, best_a, best_b, weights, o_send, e_send, o_recv, e_recv,
    local_sem, a_send, a_recv, c_send, c_recv, h_send, h_recv, p_send, p_recv,
):
    seq, grp = lax.axis_index("seq"), lax.axis_index("grp")
    core = lax.rem(grp, 2)
    z, x = seq // SIDE, lax.rem(seq, SIDE)

    def along_z(d):
        return lax.rem(z + d + SIDE, SIDE) * SIDE + x

    def along_x(d):
        return z * SIDE + lax.rem(x + d + SIDE, SIDE)

    def cache_peer(d):
        return (1 - core) * along_z(d) + core * along_x(d)

    def head_peer(d):
        return core * along_z(d) + (1 - core) * along_x(d)

    def remote(src, dst, send, recv, peer):
        return pltpu.make_async_remote_copy(
            src_ref=src, dst_ref=dst, send_sem=send, recv_sem=recv,
            device_id=(peer, grp), device_id_type=MESH,
        )

    barrier = pltpu.get_barrier_semaphore()
    for d in range(1, SEQ):
        pl.semaphore_signal(
            barrier, inc=1, device_id=(lax.rem(seq + d, SEQ), grp), device_id_type=MESH
        )

    own_keys = [
        pltpu.make_async_copy(
            cache_ref.at[:, pl.ds(h * HALF, HALF)], k_all.at[h, pl.ds(0, KEY)], local_sem.at[4 * h]
        )
        for h in range(2)
    ]
    own_uk = pltpu.make_async_copy(uk_hbm, uk, local_sem.at[1])
    own_uv = pltpu.make_async_copy(uv_hbm, uv, local_sem.at[2])
    for c in own_keys:
        c.start()
    own_uk.start()
    own_uv.start()

    rows8[...] = jnp.zeros(rows8.shape, F32)
    rows8[0:4, :] = query_ref[...].astype(F32)
    rows8[4:5, :] = dec_query_ref[...].astype(F32)
    kv8[...] = jnp.zeros(kv8.shape, F32)
    kv8[0:4, 0:KEY] = span_kv_ref[...].astype(F32)
    kv8[4:5, 0:KEY] = dec_kv_ref[...].astype(F32)
    kv_out[...] = kv8[...].astype(BF16)
    for s in range(SEQ):
        a_out[s] = rows8[:, s * SLICE : (s + 1) * SLICE].astype(BF16)
    a_in[seq] = a_out[seq]
    kv_in[seq] = kv_out[...]

    pl.semaphore_wait(barrier, SEQ - 1)

    exchange, exchange_kv = [], []
    for d in range(1, SEQ):
        peer = lax.rem(seq + d, SEQ)
        exchange.append(remote(a_out.at[peer], a_in.at[seq], a_send.at[d - 1], a_recv.at[d - 1], peer))
        exchange_kv.append(
            remote(kv_out, kv_in.at[seq], a_send.at[SEQ + d - 2], a_recv.at[SEQ + d - 2], peer)
        )
    for c in exchange:
        c.start()

    def ring(halves, send, recv, peer_of):
        count = len(halves(0, 0))

        def pair(i, src_slot, dst_slot, h, peer):
            src, dst = halves(src_slot, h), halves(dst_slot, h)
            return [
                remote(src[k], dst[k], send.at[count * i + k], recv.at[count * i + k], peer)
                for k in range(count)
            ]

        up, down = peer_of(1), peer_of(-1)
        first_up = pair(0, 0, 1, 0, up)
        first_down = pair(1, 0, 3, 1, down)
        second_up = pair(2, 0, 1, 1, up)
        second_down = pair(3, 0, 3, 0, down)
        onward_up = pair(4, 1, 2, 0, up)
        onward_down = pair(5, 3, 2, 1, down)
        return first_up, first_down, second_up, second_down, onward_up, onward_down

    def key_half(slot, h):
        return [k_all.at[PIECES.index((slot, h)), pl.ds(0, KEY)]]

    def query_half(slot, h):
        return [q_all.at[2 * slot + h, pl.ds(0, BAND), pl.ds(0, DC)], qr_all.at[2 * slot + h]]

    def start(*groups):
        for g in groups:
            for c in g:
                c.start()

    def arrived(*groups):
        for g in groups:
            for c in g:
                c.wait_recv()

    def sent(*groups):
        for g in groups:
            for c in g:
                c.wait_send()

    cring = ring(key_half, c_send, c_recv, cache_peer)
    hring = ring(query_half, h_send, h_recv, head_peer)

    def unpack_keys(block):
        for piece in (2 * block, 2 * block + 1):
            k_all[piece, KEY:WIDE, :] = k_all[piece, DC:KEY, :]

    def unpack_queries(band):
        for p in range(HEADS // 4):
            both = qr_all[band, COUNT * p : COUNT * (p + 1), :].astype(F32)
            mask = lane_mask(both.shape)
            at = 2 * COUNT * p
            q_all[band, at : at + COUNT, DC:WIDE] = jnp.where(mask, both, 0.0).astype(BF16)
            q_all[band, at + COUNT : at + 2 * COUNT, DC:WIDE] = jnp.where(mask, 0.0, both).astype(BF16)

    for c in own_keys:
        c.wait()
    for c in exchange_kv:
        c.start()
    start(cring[0], cring[1])
    unpack_keys(0)
    peak[...] = jnp.full(peak.shape, LOW, F32)
    total[...] = jnp.zeros(total.shape, F32)
    acc[...] = jnp.zeros(acc.shape, F32)
    e_send[...] = jnp.zeros(e_send.shape, F32)

    prow = lax.broadcasted_iota(jnp.int32, (COUNT, 128), 0)
    pcol = lax.broadcasted_iota(jnp.int32, (COUNT, 128), 1)
    place = jnp.where(prow < SPAN, 8 * (prow // 4) + lax.rem(prow, 4), 8 * (prow - SPAN) + 4)
    order = jnp.where(pcol == place, 1.0, 0.0).astype(BF16)
    own_uk.wait()
    for c in exchange:
        c.wait_recv()
    got = a_in[...].astype(F32).reshape(8 * SEQ, SLICE).astype(BF16)
    got = dot(order, got)
    for p in range(HEADS // 2):
        at = 3 * 128 * p
        t0, t1, t2 = (got[:, at + 128 * i : at + 128 * (i + 1)] for i in range(3))
        mask = lane_mask(t0.shape)
        nope = t0.astype(BF16)
        swapped = jnp.where(mask, t2, t1).astype(BF16)
        band, pair = p // 2, p % 2
        qr_all[band, COUNT * pair : COUNT * (pair + 1), :] = jnp.where(mask, t1, t2).astype(BF16)
        weight = uk[2 * p + 1]
        weight = jnp.concatenate([weight[DR:], weight[:DR]], axis=0)
        row0 = 2 * COUNT * pair
        q_all[band, row0 : row0 + COUNT, 0:DC] = dot(nope, uk[2 * p]).astype(BF16)
        q_all[band, row0 + COUNT : row0 + 2 * COUNT, 0:DC] = dot(swapped, weight).astype(BF16)
        if p == 1:
            start(hring[0])
        if p == 3:
            start(hring[1], hring[2], hring[3])
    unpack_queries(0)
    unpack_queries(1)

    for c in exchange_kv:
        c.wait_recv()
    kv_rows = kv_in[...].astype(F32).reshape(8 * SEQ, WIDE).astype(BF16)
    kv_rows = dot(order, kv_rows).astype(BF16)
    k_own[...] = jnp.zeros(k_own.shape, BF16)
    k_own[0:COUNT, 0:DC] = kv_rows[:, 0:DC]
    k_own[0:COUNT, DC:WIDE] = dot(kv_rows[:, DC:WIDE], doubled()).astype(BF16)

    def scores(band, block, out, best):
        top = None
        for side in range(2):
            slot = pick([PIECES[2 * b + side][0] for b in range(SIDE)], block)
            half = pick([PIECES[2 * b + side][1] for b in range(SIDE)], block)
            fill = fill_ref[cache_peer(-slot)] - half * HALF
            for j in range(0, HALF, CHUNK):
                s = dot(q_all[band], k_all[2 * block + side, :, j : j + CHUNK])
                local = lax.broadcasted_iota(jnp.int32, (1, CHUNK), 1) + j
                s = jnp.where(local < fill, s, LOW)
                out[:, side * HALF + j : side * HALF + j + CHUNK] = s
                for u in range(0, CHUNK, 128):
                    top = s[:, u : u + 128] if top is None else jnp.maximum(top, s[:, u : u + 128])
                yield
        best[...] = top

    def attend(band, block, now, later, ahead):
        score, best = now
        old = peak[band]
        top = jnp.maximum(old, jnp.max(best[...], axis=1, keepdims=True))
        keep = jnp.exp2((old - top) * SCALE2)
        add = None
        nxt = scores(*ahead, *later)
        for j in range(POS // CHUNK):
            next(nxt)
            at = slice(j * CHUNK, (j + 1) * CHUNK)
            e = jnp.exp2((score[:, at] - top) * SCALE2)
            weights[:, at] = e.astype(BF16)
            for u in range(0, CHUNK, 128):
                add = e[:, u : u + 128] if add is None else add + e[:, u : u + 128]
        next(nxt, None)
        out = dot_t(weights[:, 0:HALF], k_all[2 * block, 0:DC, :])
        out += dot_t(weights[:, HALF:POS], k_all[2 * block + 1, 0:DC, :])
        peak[band] = top
        total[band] = total[band] * keep + jnp.sum(add, axis=1, keepdims=True)
        acc[band] = acc[band] * keep + out

    eye = lax.broadcasted_iota(jnp.int32, (64, 128), 0) == lax.broadcasted_iota(jnp.int32, (64, 128), 1)

    def finish(band):
        t = total[band]
        o_send[band - 2] = (acc[band] * (1.0 / t)).astype(BF16)
        level = peak[band] * SCALE2 + jnp.log2(t)
        for i in range(BAND // 64):
            square = jnp.broadcast_to(level[64 * i : 64 * (i + 1)], (64, 128))
            e_send[band - 2, i : i + 1, :] = jnp.sum(jnp.where(eye, square, 0.0), axis=0, keepdims=True)

    def back(band):
        peer, i = head_peer(-(band // 2)), band - 2
        return [
            remote(o_send.at[i], o_recv.at[i], p_send.at[2 * i], p_recv.at[2 * i], peer),
            remote(e_send.at[i], e_recv.at[i], p_send.at[2 * i + 1], p_recv.at[2 * i + 1], peer),
        ]

    qrow = lax.broadcasted_iota(jnp.int32, (COUNT, 128), 0)
    kcol = lax.broadcasted_iota(jnp.int32, (COUNT, 128), 1)
    limit = jnp.where(qrow < SPAN, qrow + 1, 0)
    for r in range(ROWS):
        limit = jnp.where(qrow == SPAN + r, dlen_ref[r], limit)
    seen = (kcol < limit) | ((qrow >= SPAN) & (kcol == qrow))
    hidden = jnp.where(seen, 0.0, 1.0)
    hidden = jnp.concatenate([hidden] * (HEADS // 2), axis=0)
    for band in range(2):
        s = jnp.where(hidden > 0.5, LOW, dot_t(q_all[band], k_own[...]))
        top = jnp.max(s, axis=1, keepdims=True)
        e = jnp.exp2((s - top) * SCALE2)
        peak[band] = top
        total[band] = jnp.sum(e, axis=1, keepdims=True)
        acc[band] = dot(e.astype(BF16), k_own[:, 0:DC])

    target = jnp.where(owner_ref[...] == seq, slot_ref[...], -1)
    span_rows = kv_rows[0:SPAN, 0:KEY]

    @pl.loop(0, POS // 256)
    def _(i):
        piece = i // 2
        local = lax.broadcasted_iota(jnp.int32, (256, SPAN), 0) + i * 256
        hot = jnp.where(local == target, 1.0, 0.0).astype(BF16)
        put = lax.dot_general(span_rows, hot, (((0,), (1,)), ((), ())), preferred_element_type=F32)
        any_hot = dot_t(jnp.ones((8, SPAN), BF16), hot)[0:1] > 0.5
        at = pl.ds(pl.multiple_of(lax.rem(i, 2) * 256, 256), 256)
        old = k_all[piece, 0:KEY, at].astype(F32)
        newc[:, pl.ds(pl.multiple_of(i * 256, 256), 256)] = jnp.where(any_hot, put, old).astype(BF16)

    put_cache = pltpu.make_async_copy(newc, newc_hbm, local_sem.at[3])
    put_cache.start()

    def before(i):
        @pl.when(i == 1)
        def _():
            arrived(hring[0], hring[1])
            start(hring[4], hring[5])
            unpack_queries(2)
            unpack_queries(7)

        @pl.when(i == 3)
        def _():
            arrived(hring[2], hring[3])
            start(cring[2], cring[3])
            unpack_queries(3)
            unpack_queries(6)

        @pl.when(i == 5)
        def _():
            arrived(hring[4], hring[5])
            unpack_queries(4)
            unpack_queries(5)

        @pl.when(i == 7)
        def _():
            arrived(cring[0], cring[1])
            start(cring[4], cring[5])
            unpack_keys(1)

        @pl.when(i == 13)
        def _():
            arrived(cring[2], cring[3])
            unpack_keys(2)

        @pl.when(i == 19)
        def _():
            arrived(cring[4], cring[5])
            unpack_keys(3)

    def after(i, band):
        @pl.when((i >= FINISH) & (i < FINISH + 6))
        def _():
            finish(band)
            start(back(band))

    a, b = (score_a, best_a), (score_b, best_b)
    for _ in scores(0, 0, *a):
        pass

    def step(i, now, later):
        before(i)
        band, ks = pick(ORDER_BAND, i), pick(ORDER_KEYS, i)
        ahead = jnp.minimum(i + 1, STEPS - 1)
        attend(band, ks, now, later, (pick(ORDER_BAND, ahead), pick(ORDER_KEYS, ahead)))
        after(i, band)

    @pl.loop(0, STEPS // 2)
    def _(i):
        step(2 * i, a, b)
        step(2 * i + 1, b, a)

    own_uv.wait()
    for half in range(2):
        levels = []
        for s in range(1, SIDE):
            i = 2 * s + half - 2
            arrived(back(i + 2))
            column = []
            for j in range(BAND // 64):
                square = jnp.broadcast_to(e_recv[i, j : j + 1, :], (64, 128))
                column.append(jnp.sum(jnp.where(eye, square, 0.0), axis=1, keepdims=True))
            levels.append(jnp.concatenate(column, axis=0))
        own_level = peak[half] * SCALE2 + jnp.log2(total[half])
        top = own_level
        for level in levels:
            top = jnp.maximum(top, level)
        weight = jnp.exp2(own_level - top)
        shares = [jnp.exp2(level - top) for level in levels]
        norm = 1.0 / (weight + shares[0] + shares[1] + shares[2])
        first = weight * norm / total[half]
        shares = [share * norm for share in shares]
        for h in range(HEADS // 2):
            rows = slice(COUNT * h, COUNT * (h + 1))
            latent = acc[half, rows, :] * first[rows]
            for s in range(SIDE - 1):
                latent = latent + o_recv[2 * s + half, rows, :].astype(F32) * shares[s][rows]
            head = HEADS // 2 * half + h
            value = dot(latent.astype(BF16), uv[head])
            out_ref[:, DV * head : DV * (head + 1)] = value.astype(BF16)

    put_cache.wait()
    for c in exchange + exchange_kv:
        c.wait_send()
    sent(*cring, *hring)
    for band in range(2, 2 * SIDE):
        sent(back(band))


def hand_over(out_ref, cache_ref, span_ref, dec_ref, new_ref, out, cache, sem):
    half = KEY // 2
    ins = [pltpu.make_async_copy(out_ref, out, sem.at[0])]
    outs = [
        [
            pltpu.make_async_copy(out.at[pl.ds(0, SPAN)], span_ref, sem.at[3]),
            pltpu.make_async_copy(out.at[pl.ds(SPAN, ROWS)], dec_ref, sem.at[4]),
        ]
    ]
    for i in range(2):
        rows = pl.ds(i * half, half)
        ins.append(pltpu.make_async_copy(cache_ref.at[rows], cache.at[rows], sem.at[1 + i]))
        outs.append([pltpu.make_async_copy(cache.at[rows], new_ref.at[rows], sem.at[5 + i])])
    for c in ins:
        c.start()
    for c, then in zip(ins, outs):
        c.wait()
        for d in then:
            d.start()
    for then in outs:
        for d in then:
            d.wait()


def body(query, dec_query, cache_kv, span_kv, dec_kv, cache_fill, owner, slot, dec_len, w_uk, w_uv):
    vmem = pl.BlockSpec(memory_space=pltpu.VMEM)
    smem = pl.BlockSpec(memory_space=pltpu.SMEM)
    hbm = pl.BlockSpec(memory_space=pl.ANY)
    dma = pltpu.SemaphoreType.DMA
    shape = jax.ShapeDtypeStruct
    out, new_cache = pl.pallas_call(
        kernel,
        out_shape=(shape((COUNT, HEADS * DV), BF16), shape((KEY, POS), BF16)),
        in_specs=[vmem, vmem, vmem, vmem, hbm, smem, vmem, vmem, smem, hbm, hbm],
        out_specs=(vmem, hbm),
        scratch_shapes=[
            pltpu.VMEM((8, SEQ * SLICE), F32),
            pltpu.VMEM((8, WIDE), F32),
            pltpu.VMEM((SEQ, 8, SLICE), BF16),
            pltpu.VMEM((SEQ, 8, SLICE), BF16),
            pltpu.VMEM((8, WIDE), BF16),
            pltpu.VMEM((SEQ, 8, WIDE), BF16),
            pltpu.VMEM((2 * SIDE, BAND, WIDE), BF16),
            pltpu.VMEM((2 * SIDE, BAND // 2, 128), BF16),
            pltpu.VMEM((2 * SIDE, WIDE, HALF), BF16),
            pltpu.VMEM((128, WIDE), BF16),
            pltpu.VMEM((HEADS, DN, DC), BF16),
            pltpu.VMEM((HEADS, DC, DV), BF16),
            pltpu.VMEM((KEY, POS), BF16),
            pltpu.VMEM((2 * SIDE, BAND, DC), F32),
            pltpu.VMEM((2 * SIDE, BAND, 1), F32),
            pltpu.VMEM((2 * SIDE, BAND, 1), F32),
            pltpu.VMEM((BAND, POS), F32),
            pltpu.VMEM((BAND, POS), F32),
            pltpu.VMEM((BAND, 128), F32),
            pltpu.VMEM((BAND, 128), F32),
            pltpu.VMEM((BAND, POS), BF16),
            pltpu.VMEM((6, BAND, DC), BF16),
            pltpu.VMEM((6, 8, 128), F32),
            pltpu.VMEM((6, BAND, DC), BF16),
            pltpu.VMEM((6, 8, 128), F32),
            dma((5,)),
            dma((2 * (SEQ - 1),)),
            dma((2 * (SEQ - 1),)),
            dma((6,)),
            dma((6,)),
            dma((12,)),
            dma((12,)),
            dma((12,)),
            dma((12,)),
        ],
        compiler_params=pltpu.CompilerParams(
            collective_id=0, has_side_effects=True, vmem_limit_bytes=56 * 2**20
        ),
        cost_estimate=pl.CostEstimate(
            flops=2 * STEPS * BAND * POS * (KEY + DC),
            bytes_accessed=8 * 2**20,
            transcendentals=STEPS * BAND * POS,
        ),
    )(
        query, dec_query, span_kv, dec_kv, cache_kv.T, cache_fill,
        owner.reshape(1, SPAN), slot.reshape(1, SPAN), dec_len, w_uk, w_uv,
    )
    span_out, dec_out, new_cache = pl.pallas_call(
        hand_over,
        out_shape=(
            shape((SPAN, HEADS * DV), BF16),
            shape((ROWS, HEADS * DV), BF16),
            shape((KEY, POS), BF16),
        ),
        in_specs=[hbm, hbm],
        out_specs=(hbm, hbm, hbm),
        scratch_shapes=[
            pltpu.VMEM((COUNT, HEADS * DV), BF16),
            pltpu.VMEM((KEY, POS), BF16),
            dma((7,)),
        ],
        compiler_params=pltpu.CompilerParams(vmem_limit_bytes=60 * 2**20),
        cost_estimate=pl.CostEstimate(flops=0, bytes_accessed=3 * 2**20, transcendentals=0),
    )(out, new_cache)
    return span_out, dec_out, new_cache.T


def solution(mesh):
    in_specs = (
        P(("grp", "seq"), None),
        P(("grp", "seq"), None),
        P(("grp", "seq"), None),
        P(("grp", "seq"), None),
        P(("grp", "seq"), None),
        P("grp"),
        P("grp"),
        P("grp"),
        P("grp"),
        P("seq", None, None),
        P("seq", None, None),
    )
    out_specs = (P("grp", "seq"), P("grp", "seq"), P(("grp", "seq"), None))
    return jax.shard_map(body, mesh=mesh, in_specs=in_specs, out_specs=out_specs, check_vma=False)
```

```python
import functools
import math

import jax
import jax.numpy as jnp
from jax import lax
from jax.experimental import pallas as pl
from jax.experimental.pallas import tpu as pltpu
from jax.sharding import PartitionSpec as P

MESH = pl.DeviceIdType.MESH
F32 = jnp.float32
BF16 = jnp.bfloat16

SIDE = 4
SEQ = SIDE * SIDE
HEADS = 8
DN = 128
DR = 64
DC = 512
DV = 128
KEY = DC + DR
WIDE = DC + 128
POS = 1024
SPAN = 64
ROWS = 16
COUNT = SPAN + ROWS
BAND = HEADS // 2 * COUNT
SLICE = HEADS * (DN + DR)
CHUNK = 256

SCALE2 = 0.1353 * math.log2(math.e)
LOW = -1e30

PIECES = ((0, 0), (0, 1), (1, 0), (3, 1), (1, 1), (3, 0), (2, 0), (2, 1))
HALF = POS // 2
ORDER_BAND = (0, 1, 0, 1, 2, 7, 2, 7, 3, 6, 3, 6, 4, 5, 4, 5) + (4, 5, 3, 6, 2, 7) * 2 + (0, 1) * 2
ORDER_KEYS = (0, 0, 1, 1) * 4 + (2,) * 6 + (3,) * 6 + (2, 2, 3, 3)
STEPS = len(ORDER_BAND)
FINISH = 22


def dot(a, b):
    return jnp.dot(a, b, preferred_element_type=F32)


def dot_t(a, b):
    return lax.dot_general(a, b, (((1,), (1,)), ((), ())), preferred_element_type=F32)


def lane_mask(shape):
    return lax.broadcasted_iota(jnp.int32, shape, len(shape) - 1) < DR


def doubled():
    row = lax.broadcasted_iota(jnp.int32, (128, 128), 0)
    col = lax.broadcasted_iota(jnp.int32, (128, 128), 1)
    return jnp.where(row == lax.rem(col, DR), 1.0, 0.0).astype(BF16)


def pick(table, i):
    word = None
    for lo in reversed(range(0, len(table), 8)):
        packed = sum(entry << (4 * at) for at, entry in enumerate(table[lo : lo + 8]))
        word = jnp.int32(packed) if word is None else jnp.where(i < lo + 8, jnp.int32(packed), word)
    return lax.shift_right_logical(word, 4 * lax.rem(i, 8)) & 7


def kernel(
    query_ref, dec_query_ref, span_kv_ref, dec_kv_ref, cache_ref, fill_ref, owner_ref, slot_ref, dlen_ref,
    uk_hbm, uv_hbm,
    out_ref, newc_hbm,
    rows8, kv8, a_out, a_in, kv_out, kv_in, q_all, qr_all, k_all, k_own, uk, uv, newc,
    acc, peak, total, score_a, score_b, best_a, best_b, weights, o_send, e_send, o_recv, e_recv,
    local_sem, a_send, a_recv, c_send, c_recv, h_send, h_recv, p_send, p_recv,
):
    seq, grp = lax.axis_index("seq"), lax.axis_index("grp")
    core = lax.rem(grp, 2)
    z, x = seq // SIDE, lax.rem(seq, SIDE)

    def along_z(d):
        return lax.rem(z + d + SIDE, SIDE) * SIDE + x

    def along_x(d):
        return z * SIDE + lax.rem(x + d + SIDE, SIDE)

    def cache_peer(d):
        return (1 - core) * along_z(d) + core * along_x(d)

    def head_peer(d):
        return core * along_z(d) + (1 - core) * along_x(d)

    def remote(src, dst, send, recv, peer):
        return pltpu.make_async_remote_copy(
            src_ref=src, dst_ref=dst, send_sem=send, recv_sem=recv,
            device_id=(peer, grp), device_id_type=MESH,
        )

    barrier = pltpu.get_barrier_semaphore()
    for d in range(1, SEQ):
        pl.semaphore_signal(
            barrier, inc=1, device_id=(lax.rem(seq + d, SEQ), grp), device_id_type=MESH
        )

    own_keys = [
        pltpu.make_async_copy(
            cache_ref.at[:, pl.ds(h * HALF, HALF)], k_all.at[h, pl.ds(0, KEY)], local_sem.at[4 * h]
        )
        for h in range(2)
    ]
    own_uk = pltpu.make_async_copy(uk_hbm, uk, local_sem.at[1])
    own_uv = pltpu.make_async_copy(uv_hbm, uv, local_sem.at[2])
    for c in own_keys:
        c.start()
    own_uk.start()
    own_uv.start()

    rows8[...] = jnp.zeros(rows8.shape, F32)
    rows8[0:4, :] = query_ref[...].astype(F32)
    rows8[4:5, :] = dec_query_ref[...].astype(F32)
    kv8[...] = jnp.zeros(kv8.shape, F32)
    kv8[0:4, 0:KEY] = span_kv_ref[...].astype(F32)
    kv8[4:5, 0:KEY] = dec_kv_ref[...].astype(F32)
    kv_out[...] = kv8[...].astype(BF16)
    for s in range(SEQ):
        a_out[s] = rows8[:, s * SLICE : (s + 1) * SLICE].astype(BF16)
    a_in[seq] = a_out[seq]
    kv_in[seq] = kv_out[...]

    pl.semaphore_wait(barrier, SEQ - 1)

    exchange, exchange_kv = [], []
    for d in range(1, SEQ):
        peer = lax.rem(seq + d, SEQ)
        exchange.append(remote(a_out.at[peer], a_in.at[seq], a_send.at[d - 1], a_recv.at[d - 1], peer))
        exchange_kv.append(
            remote(kv_out, kv_in.at[seq], a_send.at[SEQ + d - 2], a_recv.at[SEQ + d - 2], peer)
        )
    for c in exchange:
        c.start()

    def ring(halves, send, recv, peer_of):
        count = len(halves(0, 0))

        def pair(i, src_slot, dst_slot, h, peer):
            src, dst = halves(src_slot, h), halves(dst_slot, h)
            return [
                remote(src[k], dst[k], send.at[count * i + k], recv.at[count * i + k], peer)
                for k in range(count)
            ]

        up, down = peer_of(1), peer_of(-1)
        first_up = pair(0, 0, 1, 0, up)
        first_down = pair(1, 0, 3, 1, down)
        second_up = pair(2, 0, 1, 1, up)
        second_down = pair(3, 0, 3, 0, down)
        onward_up = pair(4, 1, 2, 0, up)
        onward_down = pair(5, 3, 2, 1, down)
        return first_up, first_down, second_up, second_down, onward_up, onward_down

    def key_half(slot, h):
        return [k_all.at[PIECES.index((slot, h)), pl.ds(0, KEY)]]

    def query_half(slot, h):
        return [q_all.at[2 * slot + h, pl.ds(0, BAND), pl.ds(0, DC)], qr_all.at[2 * slot + h]]

    def start(*groups):
        for g in groups:
            for c in g:
                c.start()

    def arrived(*groups):
        for g in groups:
            for c in g:
                c.wait_recv()

    def sent(*groups):
        for g in groups:
            for c in g:
                c.wait_send()

    cring = ring(key_half, c_send, c_recv, cache_peer)
    hring = ring(query_half, h_send, h_recv, head_peer)

    def unpack_keys(block):
        for piece in (2 * block, 2 * block + 1):
            k_all[piece, KEY:WIDE, :] = k_all[piece, DC:KEY, :]

    def unpack_queries(band):
        for p in range(HEADS // 4):
            both = qr_all[band, COUNT * p : COUNT * (p + 1), :].astype(F32)
            mask = lane_mask(both.shape)
            at = 2 * COUNT * p
            q_all[band, at : at + COUNT, DC:WIDE] = jnp.where(mask, both, 0.0).astype(BF16)
            q_all[band, at + COUNT : at + 2 * COUNT, DC:WIDE] = jnp.where(mask, 0.0, both).astype(BF16)

    for c in own_keys:
        c.wait()
    for c in exchange_kv:
        c.start()
    start(cring[0], cring[1])
    unpack_keys(0)
    peak[...] = jnp.full(peak.shape, LOW, F32)
    total[...] = jnp.zeros(total.shape, F32)
    acc[...] = jnp.zeros(acc.shape, F32)
    e_send[...] = jnp.zeros(e_send.shape, F32)

    prow = lax.broadcasted_iota(jnp.int32, (COUNT, 128), 0)
    pcol = lax.broadcasted_iota(jnp.int32, (COUNT, 128), 1)
    place = jnp.where(prow < SPAN, 8 * (prow // 4) + lax.rem(prow, 4), 8 * (prow - SPAN) + 4)
    order = jnp.where(pcol == place, 1.0, 0.0).astype(BF16)
    own_uk.wait()
    for c in exchange:
        c.wait_recv()
    got = a_in[...].astype(F32).reshape(8 * SEQ, SLICE).astype(BF16)
    got = dot(order, got)
    for p in range(HEADS // 2):
        at = 3 * 128 * p
        t0, t1, t2 = (got[:, at + 128 * i : at + 128 * (i + 1)] for i in range(3))
        mask = lane_mask(t0.shape)
        nope = t0.astype(BF16)
        swapped = jnp.where(mask, t2, t1).astype(BF16)
        band, pair = p // 2, p % 2
        qr_all[band, COUNT * pair : COUNT * (pair + 1), :] = jnp.where(mask, t1, t2).astype(BF16)
        weight = uk[2 * p + 1]
        weight = jnp.concatenate([weight[DR:], weight[:DR]], axis=0)
        row0 = 2 * COUNT * pair
        q_all[band, row0 : row0 + COUNT, 0:DC] = dot(nope, uk[2 * p]).astype(BF16)
        q_all[band, row0 + COUNT : row0 + 2 * COUNT, 0:DC] = dot(swapped, weight).astype(BF16)
        if p == 1:
            start(hring[0])
        if p == 3:
            start(hring[1], hring[2], hring[3])
    unpack_queries(0)
    unpack_queries(1)

    for c in exchange_kv:
        c.wait_recv()
    kv_rows = kv_in[...].astype(F32).reshape(8 * SEQ, WIDE).astype(BF16)
    kv_rows = dot(order, kv_rows).astype(BF16)
    k_own[...] = jnp.zeros(k_own.shape, BF16)
    k_own[0:COUNT, 0:DC] = kv_rows[:, 0:DC]
    k_own[0:COUNT, DC:WIDE] = dot(kv_rows[:, DC:WIDE], doubled()).astype(BF16)

    def scores(band, block, out, best):
        top = None
        for side in range(2):
            slot = pick([PIECES[2 * b + side][0] for b in range(SIDE)], block)
            half = pick([PIECES[2 * b + side][1] for b in range(SIDE)], block)
            fill = fill_ref[cache_peer(-slot)] - half * HALF
            for j in range(0, HALF, CHUNK):
                s = dot(q_all[band], k_all[2 * block + side, :, j : j + CHUNK])
                local = lax.broadcasted_iota(jnp.int32, (1, CHUNK), 1) + j
                s = jnp.where(local < fill, s, LOW)
                out[:, side * HALF + j : side * HALF + j + CHUNK] = s
                for u in range(0, CHUNK, 128):
                    top = s[:, u : u + 128] if top is None else jnp.maximum(top, s[:, u : u + 128])
                yield
        best[...] = top

    def attend(band, block, now, later, ahead):
        score, best = now
        old = peak[band]
        top = jnp.maximum(old, jnp.max(best[...], axis=1, keepdims=True))
        keep = jnp.exp2((old - top) * SCALE2)
        add = None
        nxt = scores(*ahead, *later) if ahead is not None else iter((None,) * 4)
        for j in range(POS // CHUNK):
            next(nxt)
            at = slice(j * CHUNK, (j + 1) * CHUNK)
            e = jnp.exp2((score[:, at] - top) * SCALE2)
            weights[:, at] = e.astype(BF16)
            for u in range(0, CHUNK, 128):
                add = e[:, u : u + 128] if add is None else add + e[:, u : u + 128]
        next(nxt, None)
        out = dot_t(weights[:, 0:HALF], k_all[2 * block, 0:DC, :])
        out += dot_t(weights[:, HALF:POS], k_all[2 * block + 1, 0:DC, :])
        peak[band] = top
        total[band] = total[band] * keep + jnp.sum(add, axis=1, keepdims=True)
        acc[band] = acc[band] * keep + out

    eye = lax.broadcasted_iota(jnp.int32, (64, 128), 0) == lax.broadcasted_iota(jnp.int32, (64, 128), 1)

    def rows_to_lanes(level, ref, index):
        for i in range(BAND // 64):
            square = jnp.broadcast_to(level[64 * i : 64 * (i + 1)], (64, 128))
            ref[index, i : i + 1, :] = jnp.sum(jnp.where(eye, square, 0.0), axis=0, keepdims=True)

    def lanes_to_rows(ref, index):
        column = []
        for i in range(BAND // 64):
            square = jnp.broadcast_to(ref[index, i : i + 1, :], (64, 128))
            column.append(jnp.sum(jnp.where(eye, square, 0.0), axis=1, keepdims=True))
        return jnp.concatenate(column, axis=0)

    def back(band):
        peer, i = head_peer(jnp.where(band <= 4, -1, 1)), band - 2
        return [
            remote(o_send.at[i], o_recv.at[i], p_send.at[2 * i], p_recv.at[2 * i], peer),
            remote(e_send.at[i], e_recv.at[i], p_send.at[2 * i + 1], p_recv.at[2 * i + 1], peer),
        ]

    def finish(band):
        t = total[band]
        o_send[band - 2] = (acc[band] * (1.0 / t)).astype(BF16)
        rows_to_lanes(peak[band] * SCALE2 + jnp.log2(t), e_send, band - 2)

    def finish_both(band, other):
        arrived(back(other))
        t = total[band]
        here, there = peak[band] * SCALE2 + jnp.log2(t), lanes_to_rows(e_recv, other - 2)
        top = jnp.maximum(here, there)
        w_here, w_there = jnp.exp2(here - top), jnp.exp2(there - top)
        both = w_here + w_there
        norm = 1.0 / both
        part = acc[band] * (w_here * norm / t) + o_recv[other - 2].astype(F32) * (w_there * norm)
        o_send[band - 2] = part.astype(BF16)
        rows_to_lanes(top + jnp.log2(both), e_send, band - 2)

    qrow = lax.broadcasted_iota(jnp.int32, (COUNT, 128), 0)
    kcol = lax.broadcasted_iota(jnp.int32, (COUNT, 128), 1)
    limit = jnp.where(qrow < SPAN, qrow + 1, 0)
    for r in range(ROWS):
        limit = jnp.where(qrow == SPAN + r, dlen_ref[r], limit)
    seen = (kcol < limit) | ((qrow >= SPAN) & (kcol == qrow))
    hidden = jnp.where(seen, 0.0, 1.0)
    hidden = jnp.concatenate([hidden] * (HEADS // 2), axis=0)
    for band in range(2):
        s = jnp.where(hidden > 0.5, LOW, dot_t(q_all[band], k_own[...]))
        top = jnp.max(s, axis=1, keepdims=True)
        e = jnp.exp2((s - top) * SCALE2)
        peak[band] = top
        total[band] = jnp.sum(e, axis=1, keepdims=True)
        acc[band] = dot(e.astype(BF16), k_own[:, 0:DC])

    target = jnp.where(owner_ref[...] == seq, slot_ref[...], -1)
    span_rows = kv_rows[0:SPAN, 0:KEY]

    @pl.loop(0, POS // 256)
    def _(i):
        piece = i // 2
        local = lax.broadcasted_iota(jnp.int32, (256, SPAN), 0) + i * 256
        hot = jnp.where(local == target, 1.0, 0.0).astype(BF16)
        put = lax.dot_general(span_rows, hot, (((0,), (1,)), ((), ())), preferred_element_type=F32)
        any_hot = dot_t(jnp.ones((8, SPAN), BF16), hot)[0:1] > 0.5
        at = pl.ds(pl.multiple_of(lax.rem(i, 2) * 256, 256), 256)
        old = k_all[piece, 0:KEY, at].astype(F32)
        newc[:, pl.ds(pl.multiple_of(i * 256, 256), 256)] = jnp.where(any_hot, put, old).astype(BF16)

    put_cache = pltpu.make_async_copy(newc, newc_hbm, local_sem.at[3])
    put_cache.start()

    def event(g):
        @pl.when(g == 2)
        def _():
            arrived(cring[0], cring[1])
            unpack_keys(1)

        @pl.when(g == 4)
        def _():
            arrived(hring[0], hring[1])
            start(hring[4], hring[5])
            unpack_queries(2)
            unpack_queries(7)

        @pl.when(g == 8)
        def _():
            arrived(hring[2], hring[3])
            start(cring[2], cring[3])
            unpack_queries(3)
            unpack_queries(6)

        @pl.when(g == 12)
        def _():
            arrived(hring[4], hring[5])
            start(cring[4], cring[5])
            unpack_queries(4)
            unpack_queries(5)

        @pl.when(g == 16)
        def _():
            arrived(cring[2], cring[3])
            unpack_keys(2)

        @pl.when(g == 22)
        def _():
            arrived(cring[4], cring[5])
            unpack_keys(3)

        def leave(i):
            band = pick(ORDER_BAND, i)

            @pl.when(i < FINISH + 4)
            def _():
                finish(band)

            @pl.when(i >= FINISH + 4)
            def _():
                finish_both(band, jnp.where(band == 2, 4, 5))

            start(back(band))

        for late in (3, 2):
            i = g - late

            @pl.when((i >= FINISH) & (i < FINISH + 6) & ((late == 2) | (i > FINISH)))
            def _():
                leave(i)

    a, b = (score_a, best_a), (score_b, best_b)
    for _ in scores(0, 0, *a):
        pass

    def of(i):
        return pick(ORDER_BAND, i), pick(ORDER_KEYS, i)

    attend(0, 0, a, b, (ORDER_BAND[1], ORDER_KEYS[1]))

    @pl.loop(0, STEPS // 2 - 1)
    def _(j):
        i = 2 * j + 1
        g = i + 1

        @pl.when((g <= 4) | (g == 8) | (g == 12) | (g == 16) | (g >= FINISH))
        def _():
            event(g)

        attend(*of(i), b, a, of(i + 1))
        attend(*of(i + 1), a, b, of(i + 2))

    attend(ORDER_BAND[-1], ORDER_KEYS[-1], b, a, None)

    own_uv.wait()
    for half in range(2):
        parts = (half, 4 + half)
        levels = []
        for i in parts:
            arrived(back(i + 2))
            levels.append(lanes_to_rows(e_recv, i))
        own_level = peak[half] * SCALE2 + jnp.log2(total[half])
        top = own_level
        for level in levels:
            top = jnp.maximum(top, level)
        weight = jnp.exp2(own_level - top)
        shares = [jnp.exp2(level - top) for level in levels]
        norm = 1.0 / (weight + shares[0] + shares[1])
        first = weight * norm / total[half]
        shares = [share * norm for share in shares]
        for h in range(HEADS // 2):
            rows = slice(COUNT * h, COUNT * (h + 1))
            latent = acc[half, rows, :] * first[rows]
            for i, share in zip(parts, shares):
                latent = latent + o_recv[i, rows, :].astype(F32) * share[rows]
            head = HEADS // 2 * half + h
            value = dot(latent.astype(BF16), uv[head])
            out_ref[:, DV * head : DV * (head + 1)] = value.astype(BF16)

    put_cache.wait()
    for c in exchange + exchange_kv:
        c.wait_send()
    sent(*cring, *hring)
    for band in range(2, 2 * SIDE):
        sent(back(band))


def hand_over(out_ref, cache_ref, span_ref, dec_ref, new_ref, out, cache, sem):
    half = KEY // 2
    ins = [pltpu.make_async_copy(out_ref, out, sem.at[0])]
    outs = [
        [
            pltpu.make_async_copy(out.at[pl.ds(0, SPAN)], span_ref, sem.at[3]),
            pltpu.make_async_copy(out.at[pl.ds(SPAN, ROWS)], dec_ref, sem.at[4]),
        ]
    ]
    for i in range(2):
        rows = pl.ds(i * half, half)
        ins.append(pltpu.make_async_copy(cache_ref.at[rows], cache.at[rows], sem.at[1 + i]))
        outs.append([pltpu.make_async_copy(cache.at[rows], new_ref.at[rows], sem.at[5 + i])])
    for c in ins:
        c.start()
    for c, then in zip(ins, outs):
        c.wait()
        for d in then:
            d.start()
    for then in outs:
        for d in then:
            d.wait()


def body(query, dec_query, cache_kv, span_kv, dec_kv, cache_fill, owner, slot, dec_len, w_uk, w_uv):
    vmem = pl.BlockSpec(memory_space=pltpu.VMEM)
    smem = pl.BlockSpec(memory_space=pltpu.SMEM)
    hbm = pl.BlockSpec(memory_space=pl.ANY)
    dma = pltpu.SemaphoreType.DMA
    shape = jax.ShapeDtypeStruct
    out, new_cache = pl.pallas_call(
        kernel,
        out_shape=(shape((COUNT, HEADS * DV), BF16), shape((KEY, POS), BF16)),
        in_specs=[vmem, vmem, vmem, vmem, hbm, smem, vmem, vmem, smem, hbm, hbm],
        out_specs=(vmem, hbm),
        scratch_shapes=[
            pltpu.VMEM((8, SEQ * SLICE), F32),
            pltpu.VMEM((8, WIDE), F32),
            pltpu.VMEM((SEQ, 8, SLICE), BF16),
            pltpu.VMEM((SEQ, 8, SLICE), BF16),
            pltpu.VMEM((8, WIDE), BF16),
            pltpu.VMEM((SEQ, 8, WIDE), BF16),
            pltpu.VMEM((2 * SIDE, BAND, WIDE), BF16),
            pltpu.VMEM((2 * SIDE, BAND // 2, 128), BF16),
            pltpu.VMEM((2 * SIDE, WIDE, HALF), BF16),
            pltpu.VMEM((128, WIDE), BF16),
            pltpu.VMEM((HEADS, DN, DC), BF16),
            pltpu.VMEM((HEADS, DC, DV), BF16),
            pltpu.VMEM((KEY, POS), BF16),
            pltpu.VMEM((2 * SIDE, BAND, DC), F32),
            pltpu.VMEM((2 * SIDE, BAND, 1), F32),
            pltpu.VMEM((2 * SIDE, BAND, 1), F32),
            pltpu.VMEM((BAND, POS), F32),
            pltpu.VMEM((BAND, POS), F32),
            pltpu.VMEM((BAND, 128), F32),
            pltpu.VMEM((BAND, 128), F32),
            pltpu.VMEM((BAND, POS), BF16),
            pltpu.VMEM((6, BAND, DC), BF16),
            pltpu.VMEM((6, 8, 128), F32),
            pltpu.VMEM((6, BAND, DC), BF16),
            pltpu.VMEM((6, 8, 128), F32),
            dma((5,)),
            dma((2 * (SEQ - 1),)),
            dma((2 * (SEQ - 1),)),
            dma((6,)),
            dma((6,)),
            dma((12,)),
            dma((12,)),
            dma((12,)),
            dma((12,)),
        ],
        compiler_params=pltpu.CompilerParams(
            collective_id=0, has_side_effects=True, vmem_limit_bytes=56 * 2**20
        ),
        cost_estimate=pl.CostEstimate(
            flops=2 * STEPS * BAND * POS * (KEY + DC),
            bytes_accessed=8 * 2**20,
            transcendentals=STEPS * BAND * POS,
        ),
    )(
        query, dec_query, span_kv, dec_kv, cache_kv.T, cache_fill,
        owner.reshape(1, SPAN), slot.reshape(1, SPAN), dec_len, w_uk, w_uv,
    )
    span_out, dec_out, new_cache = pl.pallas_call(
        hand_over,
        out_shape=(
            shape((SPAN, HEADS * DV), BF16),
            shape((ROWS, HEADS * DV), BF16),
            shape((KEY, POS), BF16),
        ),
        in_specs=[hbm, hbm],
        out_specs=(hbm, hbm, hbm),
        scratch_shapes=[
            pltpu.VMEM((COUNT, HEADS * DV), BF16),
            pltpu.VMEM((KEY, POS), BF16),
            dma((7,)),
        ],
        compiler_params=pltpu.CompilerParams(vmem_limit_bytes=60 * 2**20),
        cost_estimate=pl.CostEstimate(flops=0, bytes_accessed=3 * 2**20, transcendentals=0),
    )(out, new_cache)
    return span_out, dec_out, new_cache.T


def solution(mesh):
    in_specs = (
        P(("grp", "seq"), None),
        P(("grp", "seq"), None),
        P(("grp", "seq"), None),
        P(("grp", "seq"), None),
        P(("grp", "seq"), None),
        P("grp"),
        P("grp"),
        P("grp"),
        P("grp"),
        P("seq", None, None),
        P("seq", None, None),
    )
    out_specs = (P("grp", "seq"), P("grp", "seq"), P(("grp", "seq"), None))
    return jax.shard_map(body, mesh=mesh, in_specs=in_specs, out_specs=out_specs, check_vma=False)
```

```python
import functools
import math

import jax
import jax.numpy as jnp
from jax import lax
from jax.experimental import pallas as pl
from jax.experimental.pallas import tpu as pltpu
from jax.sharding import PartitionSpec as P

MESH = pl.DeviceIdType.MESH
F32 = jnp.float32
BF16 = jnp.bfloat16

SIDE = 4
SEQ = SIDE * SIDE
HEADS = 8
DN = 128
DR = 64
DC = 512
DV = 128
KEY = DC + DR
WIDE = DC + 128
POS = 1024
SPAN = 64
ROWS = 16
COUNT = SPAN + ROWS
BAND = HEADS // 2 * COUNT
SLICE = HEADS * (DN + DR)
CHUNK = 256

SCALE2 = 0.1353 * math.log2(math.e)
LOW = -1e30

PIECES = ((0, 0), (0, 1), (1, 0), (3, 1), (1, 1), (3, 0), (2, 0), (2, 1))
HALF = POS // 2
ORDER_BAND = (0, 1, 2, 7, 0, 1, 2, 7, 3, 6, 3, 6, 4, 5, 4, 5) + (4, 5, 3, 6, 2, 7) * 2 + (0, 1) * 2
ORDER_KEYS = (0, 0, 0, 0, 1, 1, 1, 1) + (0, 0, 1, 1) * 2 + (2,) * 6 + (3,) * 6 + (2, 2, 3, 3)
STEPS = len(ORDER_BAND)
FINISH = 22


def dot(a, b):
    return jnp.dot(a, b, preferred_element_type=F32)


def dot_t(a, b):
    return lax.dot_general(a, b, (((1,), (1,)), ((), ())), preferred_element_type=F32)


def lane_mask(shape):
    return lax.broadcasted_iota(jnp.int32, shape, len(shape) - 1) < DR


def doubled():
    row = lax.broadcasted_iota(jnp.int32, (128, 128), 0)
    col = lax.broadcasted_iota(jnp.int32, (128, 128), 1)
    return jnp.where(row == lax.rem(col, DR), 1.0, 0.0).astype(BF16)


def pick(table, i):
    word = None
    for lo in reversed(range(0, len(table), 8)):
        packed = sum(entry << (4 * at) for at, entry in enumerate(table[lo : lo + 8]))
        word = jnp.int32(packed) if word is None else jnp.where(i < lo + 8, jnp.int32(packed), word)
    return lax.shift_right_logical(word, 4 * lax.rem(i, 8)) & 7


def kernel(
    query_hbm, dec_query_hbm, span_kv_hbm, dec_kv_hbm, cache_ref, fill_ref, owner_ref, slot_ref, dlen_ref,
    uk_hbm, uv_hbm,
    out_ref, newc_hbm,
    query_ref, dec_query_ref, span_kv_ref, dec_kv_ref, q_in, dq_in, kv_in, dkv_in, q_rows, kv_rows32, q_all, qr_all, k_all, k_own, uk, uv, newc,
    acc, peak, total, score_a, score_b, best_a, best_b, weights, o_send, e_send, o_recv, e_recv,
    local_sem, a_send, a_recv, c_send, c_recv, h_send, h_recv, p_send, p_recv,
):
    seq, grp = lax.axis_index("seq"), lax.axis_index("grp")
    core = lax.rem(grp, 2)
    z, x = seq // SIDE, lax.rem(seq, SIDE)

    def along_z(d):
        return lax.rem(z + d + SIDE, SIDE) * SIDE + x

    def along_x(d):
        return z * SIDE + lax.rem(x + d + SIDE, SIDE)

    def cache_peer(d):
        return (1 - core) * along_z(d) + core * along_x(d)

    def head_peer(d):
        return core * along_z(d) + (1 - core) * along_x(d)

    def remote(src, dst, send, recv, peer):
        return pltpu.make_async_remote_copy(
            src_ref=src, dst_ref=dst, send_sem=send, recv_sem=recv,
            device_id=(peer, grp), device_id_type=MESH,
        )

    barrier = pltpu.get_barrier_semaphore()
    for d in range(1, SEQ):
        pl.semaphore_signal(
            barrier, inc=1, device_id=(lax.rem(seq + d, SEQ), grp), device_id_type=MESH
        )

    inputs = [
        pltpu.make_async_copy(query_hbm, query_ref, local_sem.at[5]),
        pltpu.make_async_copy(dec_query_hbm, dec_query_ref, local_sem.at[6]),
        pltpu.make_async_copy(span_kv_hbm, span_kv_ref, local_sem.at[7]),
        pltpu.make_async_copy(dec_kv_hbm, dec_kv_ref, local_sem.at[8]),
    ]
    for c in inputs:
        c.start()
    own_keys = [
        pltpu.make_async_copy(
            cache_ref.at[:, pl.ds(h * HALF, HALF)], k_all.at[h, pl.ds(0, KEY)], local_sem.at[4 * h]
        )
        for h in range(2)
    ]
    own_uk = pltpu.make_async_copy(uk_hbm, uk, local_sem.at[1])
    own_uv = pltpu.make_async_copy(uv_hbm, uv, local_sem.at[2])
    for c in own_keys:
        c.start()
    own_uk.start()
    own_uv.start()

    pl.semaphore_wait(barrier, SEQ - 1)

    def heads_of(ref, device):
        return ref.at[:, pl.ds(pl.multiple_of(device * SLICE, 128), SLICE)]

    for c in inputs:
        c.wait()
    exchange, exchange_kv = [], []
    for d in range(1, SEQ):
        peer = lax.rem(seq + d, SEQ)
        moves = (
            (heads_of(query_ref, peer), q_in, exchange),
            (heads_of(dec_query_ref, peer), dq_in, exchange),
            (span_kv_ref, kv_in, exchange_kv),
            (dec_kv_ref, dkv_in, exchange_kv),
        )
        for at, (src, dst, group) in enumerate(moves):
            i = (SEQ - 1) * at + d - 1
            group.append(remote(src, dst.at[seq], a_send.at[i], a_recv.at[i], peer))
    for c in exchange[0::2] + exchange[1::2]:
        c.start()

    def ring(halves, send, recv, peer_of):
        count = len(halves(0, 0))

        def pair(i, src_slot, dst_slot, h, peer):
            src, dst = halves(src_slot, h), halves(dst_slot, h)
            return [
                remote(src[k], dst[k], send.at[count * i + k], recv.at[count * i + k], peer)
                for k in range(count)
            ]

        up, down = peer_of(1), peer_of(-1)
        first_up = pair(0, 0, 1, 0, up)
        first_down = pair(1, 0, 3, 1, down)
        second_up = pair(2, 0, 1, 1, up)
        second_down = pair(3, 0, 3, 0, down)
        onward_up = pair(4, 1, 2, 0, up)
        onward_down = pair(5, 3, 2, 1, down)
        return first_up, first_down, second_up, second_down, onward_up, onward_down

    def key_half(slot, h):
        return [k_all.at[PIECES.index((slot, h)), pl.ds(0, KEY)]]

    def query_half(slot, h):
        return [q_all.at[2 * slot + h, pl.ds(0, BAND), pl.ds(0, DC)], qr_all.at[2 * slot + h]]

    def start(*groups):
        for g in groups:
            for c in g:
                c.start()

    def arrived(*groups):
        for g in groups:
            for c in g:
                c.wait_recv()

    def sent(*groups):
        for g in groups:
            for c in g:
                c.wait_send()

    cring = ring(key_half, c_send, c_recv, cache_peer)
    hring = ring(query_half, h_send, h_recv, head_peer)

    def unpack_keys(block):
        for piece in (2 * block, 2 * block + 1):
            k_all[piece, KEY:WIDE, :] = k_all[piece, DC:KEY, :]

    def unpack_queries(band):
        for p in range(HEADS // 4):
            both = qr_all[band, COUNT * p : COUNT * (p + 1), :].astype(F32)
            mask = lane_mask(both.shape)
            at = 2 * COUNT * p
            q_all[band, at : at + COUNT, DC:WIDE] = jnp.where(mask, both, 0.0).astype(BF16)
            q_all[band, at + COUNT : at + 2 * COUNT, DC:WIDE] = jnp.where(mask, 0.0, both).astype(BF16)

    for c in own_keys:
        c.wait()
    for c in exchange_kv[0::2] + exchange_kv[1::2]:
        c.start()
    start(cring[0], cring[1])
    mine = pl.ds(pl.multiple_of(seq * SLICE, 128), SLICE)
    q_in[seq] = query_ref[:, mine]
    dq_in[seq] = dec_query_ref[:, mine]
    kv_in[seq] = span_kv_ref[...]
    dkv_in[seq] = dec_kv_ref[...]
    unpack_keys(0)
    peak[...] = jnp.full(peak.shape, LOW, F32)
    total[...] = jnp.zeros(total.shape, F32)
    acc[...] = jnp.zeros(acc.shape, F32)
    e_send[...] = jnp.zeros(e_send.shape, F32)

    own_uk.wait()
    for c in exchange:
        c.wait_recv()
    fours = SPAN // SEQ
    for device in range(SEQ):
        q_rows[fours * device : fours * (device + 1), :] = q_in[device].astype(F32)
        q_rows[SPAN + device : SPAN + device + 1, :] = dq_in[device].astype(F32)
    got = q_rows[...]
    for p in range(HEADS // 2):
        at = 3 * 128 * p
        t0, t1, t2 = (got[:, at + 128 * i : at + 128 * (i + 1)] for i in range(3))
        mask = lane_mask(t0.shape)
        nope = t0.astype(BF16)
        swapped = jnp.where(mask, t2, t1).astype(BF16)
        band, pair = p // 2, p % 2
        qr_all[band, COUNT * pair : COUNT * (pair + 1), :] = jnp.where(mask, t1, t2).astype(BF16)
        weight = uk[2 * p + 1]
        weight = jnp.concatenate([weight[DR:], weight[:DR]], axis=0)
        row0 = 2 * COUNT * pair
        q_all[band, row0 : row0 + COUNT, 0:DC] = dot(nope, uk[2 * p]).astype(BF16)
        q_all[band, row0 + COUNT : row0 + 2 * COUNT, 0:DC] = dot(swapped, weight).astype(BF16)
        if p == 1:
            start(hring[0])
        if p == 3:
            start(hring[1], hring[2], hring[3])
    unpack_queries(0)
    unpack_queries(1)

    for c in exchange_kv:
        c.wait_recv()
    kv_rows32[...] = jnp.zeros(kv_rows32.shape, F32)
    for device in range(SEQ):
        kv_rows32[fours * device : fours * (device + 1), 0:KEY] = kv_in[device].astype(F32)
        kv_rows32[SPAN + device : SPAN + device + 1, 0:KEY] = dkv_in[device].astype(F32)
    kv_rows = kv_rows32[...].astype(BF16)
    k_own[...] = jnp.zeros(k_own.shape, BF16)
    k_own[0:COUNT, 0:DC] = kv_rows[:, 0:DC]
    k_own[0:COUNT, DC:WIDE] = dot(kv_rows[:, DC:WIDE], doubled()).astype(BF16)

    def scores(band, block, out, best):
        top = None
        for side in range(2):
            slot = pick([PIECES[2 * b + side][0] for b in range(SIDE)], block)
            half = pick([PIECES[2 * b + side][1] for b in range(SIDE)], block)
            fill = fill_ref[cache_peer(-slot)] - half * HALF
            for j in range(0, HALF, CHUNK):
                s = dot(q_all[band], k_all[2 * block + side, :, j : j + CHUNK])
                local = lax.broadcasted_iota(jnp.int32, (1, CHUNK), 1) + j
                s = jnp.where(local < fill, s, LOW)
                out[:, side * HALF + j : side * HALF + j + CHUNK] = s
                for u in range(0, CHUNK, 128):
                    top = s[:, u : u + 128] if top is None else jnp.maximum(top, s[:, u : u + 128])
                yield
        best[...] = top

    def attend(band, block, now, later, ahead):
        score, best = now
        old = peak[band]
        top = jnp.maximum(old, jnp.max(best[...], axis=1, keepdims=True))
        keep = jnp.exp2((old - top) * SCALE2)
        add = None
        nxt = scores(*ahead, *later) if ahead is not None else iter((None,) * 4)
        for j in range(POS // CHUNK):
            next(nxt)
            at = slice(j * CHUNK, (j + 1) * CHUNK)
            e = jnp.exp2((score[:, at] - top) * SCALE2)
            weights[:, at] = e.astype(BF16)
            for u in range(0, CHUNK, 128):
                add = e[:, u : u + 128] if add is None else add + e[:, u : u + 128]
        next(nxt, None)
        out = dot_t(weights[:, 0:HALF], k_all[2 * block, 0:DC, :])
        out += dot_t(weights[:, HALF:POS], k_all[2 * block + 1, 0:DC, :])
        peak[band] = top
        total[band] = total[band] * keep + jnp.sum(add, axis=1, keepdims=True)
        acc[band] = acc[band] * keep + out

    eye = lax.broadcasted_iota(jnp.int32, (64, 128), 0) == lax.broadcasted_iota(jnp.int32, (64, 128), 1)

    def rows_to_lanes(level, ref, index):
        for i in range(BAND // 64):
            square = jnp.broadcast_to(level[64 * i : 64 * (i + 1)], (64, 128))
            ref[index, i : i + 1, :] = jnp.sum(jnp.where(eye, square, 0.0), axis=0, keepdims=True)

    def lanes_to_rows(ref, index):
        column = []
        for i in range(BAND // 64):
            square = jnp.broadcast_to(ref[index, i : i + 1, :], (64, 128))
            column.append(jnp.sum(jnp.where(eye, square, 0.0), axis=1, keepdims=True))
        return jnp.concatenate(column, axis=0)

    def back(band):
        peer, i = head_peer(jnp.where(band <= 4, -1, 1)), band - 2
        return [
            remote(o_send.at[i], o_recv.at[i], p_send.at[2 * i], p_recv.at[2 * i], peer),
            remote(e_send.at[i], e_recv.at[i], p_send.at[2 * i + 1], p_recv.at[2 * i + 1], peer),
        ]

    def finish(band):
        t = total[band]
        o_send[band - 2] = (acc[band] * (1.0 / t)).astype(BF16)
        rows_to_lanes(peak[band] * SCALE2 + jnp.log2(t), e_send, band - 2)

    def finish_both(band, other):
        arrived(back(other))
        t = total[band]
        here, there = peak[band] * SCALE2 + jnp.log2(t), lanes_to_rows(e_recv, other - 2)
        top = jnp.maximum(here, there)
        w_here, w_there = jnp.exp2(here - top), jnp.exp2(there - top)
        both = w_here + w_there
        norm = 1.0 / both
        part = acc[band] * (w_here * norm / t) + o_recv[other - 2].astype(F32) * (w_there * norm)
        o_send[band - 2] = part.astype(BF16)
        rows_to_lanes(top + jnp.log2(both), e_send, band - 2)

    qrow = lax.broadcasted_iota(jnp.int32, (COUNT, 128), 0)
    kcol = lax.broadcasted_iota(jnp.int32, (COUNT, 128), 1)
    limit = jnp.where(qrow < SPAN, qrow + 1, 0)
    for r in range(ROWS):
        limit = jnp.where(qrow == SPAN + r, dlen_ref[r], limit)
    seen = (kcol < limit) | ((qrow >= SPAN) & (kcol == qrow))
    hidden = jnp.where(seen, 0.0, 1.0)
    hidden = jnp.concatenate([hidden] * (HEADS // 2), axis=0)
    for band in range(2):
        s = jnp.where(hidden > 0.5, LOW, dot_t(q_all[band], k_own[...]))
        top = jnp.max(s, axis=1, keepdims=True)
        e = jnp.exp2((s - top) * SCALE2)
        peak[band] = top
        total[band] = jnp.sum(e, axis=1, keepdims=True)
        acc[band] = dot(e.astype(BF16), k_own[:, 0:DC])

    target = jnp.where(owner_ref[...] == seq, slot_ref[...], -1)
    span_rows = kv_rows[0:SPAN, 0:KEY]

    @pl.loop(0, POS // 256)
    def _(i):
        piece = i // 2
        local = lax.broadcasted_iota(jnp.int32, (256, SPAN), 0) + i * 256
        hot = jnp.where(local == target, 1.0, 0.0).astype(BF16)
        put = lax.dot_general(span_rows, hot, (((0,), (1,)), ((), ())), preferred_element_type=F32)
        any_hot = dot_t(jnp.ones((8, SPAN), BF16), hot)[0:1] > 0.5
        at = pl.ds(pl.multiple_of(lax.rem(i, 2) * 256, 256), 256)
        old = k_all[piece, 0:KEY, at].astype(F32)
        newc[:, pl.ds(pl.multiple_of(i * 256, 256), 256)] = jnp.where(any_hot, put, old).astype(BF16)

    put_cache = pltpu.make_async_copy(newc, newc_hbm, local_sem.at[3])
    put_cache.start()

    def event(g):
        @pl.when(g == 4)
        def _():
            arrived(cring[0], cring[1])
            unpack_keys(1)

        @pl.when(g == 2)
        def _():
            arrived(hring[0], hring[1])
            start(hring[4], hring[5])
            unpack_queries(2)
            unpack_queries(7)

        @pl.when(g == 8)
        def _():
            arrived(hring[2], hring[3])
            start(cring[2], cring[3])
            unpack_queries(3)
            unpack_queries(6)

        @pl.when(g == 12)
        def _():
            arrived(hring[4], hring[5])
            start(cring[4], cring[5])
            unpack_queries(4)
            unpack_queries(5)

        @pl.when(g == 16)
        def _():
            arrived(cring[2], cring[3])
            unpack_keys(2)

        @pl.when(g == 22)
        def _():
            arrived(cring[4], cring[5])
            unpack_keys(3)

        def leave(i):
            band = pick(ORDER_BAND, i)

            @pl.when(i < FINISH + 4)
            def _():
                finish(band)

            @pl.when(i >= FINISH + 4)
            def _():
                finish_both(band, jnp.where(band == 2, 4, 5))

            start(back(band))

        for late in (3, 2):
            i = g - late

            @pl.when((i >= FINISH) & (i < FINISH + 6) & ((late == 2) | (i > FINISH)))
            def _():
                leave(i)

    a, b = (score_a, best_a), (score_b, best_b)
    for _ in scores(0, 0, *a):
        pass

    def of(i):
        return pick(ORDER_BAND, i), pick(ORDER_KEYS, i)

    attend(0, 0, a, b, (ORDER_BAND[1], ORDER_KEYS[1]))

    @pl.loop(0, STEPS // 2 - 1)
    def _(j):
        i = 2 * j + 1
        g = i + 1

        @pl.when((g <= 4) | (g == 8) | (g == 12) | (g == 16) | (g >= FINISH))
        def _():
            event(g)

        attend(*of(i), b, a, of(i + 1))
        attend(*of(i + 1), a, b, of(i + 2))

    attend(ORDER_BAND[-1], ORDER_KEYS[-1], b, a, None)

    own_uv.wait()
    for half in range(2):
        parts = (half, 4 + half)
        levels = []
        for i in parts:
            arrived(back(i + 2))
            levels.append(lanes_to_rows(e_recv, i))
        own_level = peak[half] * SCALE2 + jnp.log2(total[half])
        top = own_level
        for level in levels:
            top = jnp.maximum(top, level)
        weight = jnp.exp2(own_level - top)
        shares = [jnp.exp2(level - top) for level in levels]
        norm = 1.0 / (weight + shares[0] + shares[1])
        first = weight * norm / total[half]
        shares = [share * norm for share in shares]
        for h in range(HEADS // 2):
            rows = slice(COUNT * h, COUNT * (h + 1))
            latent = acc[half, rows, :] * first[rows]
            for i, share in zip(parts, shares):
                latent = latent + o_recv[i, rows, :].astype(F32) * share[rows]
            head = HEADS // 2 * half + h
            value = dot(latent.astype(BF16), uv[head])
            out_ref[:, DV * head : DV * (head + 1)] = value.astype(BF16)

    put_cache.wait()
    for c in exchange + exchange_kv:
        c.wait_send()
    sent(*cring, *hring)
    for band in range(2, 2 * SIDE):
        sent(back(band))


def hand_over(out_ref, cache_ref, span_ref, dec_ref, new_ref, out, cache, sem):
    half = KEY // 2
    ins = [pltpu.make_async_copy(out_ref, out, sem.at[0])]
    outs = [
        [
            pltpu.make_async_copy(out.at[pl.ds(0, SPAN)], span_ref, sem.at[3]),
            pltpu.make_async_copy(out.at[pl.ds(SPAN, ROWS)], dec_ref, sem.at[4]),
        ]
    ]
    for i in range(2):
        rows = pl.ds(i * half, half)
        ins.append(pltpu.make_async_copy(cache_ref.at[rows], cache.at[rows], sem.at[1 + i]))
        outs.append([pltpu.make_async_copy(cache.at[rows], new_ref.at[rows], sem.at[5 + i])])
    for c in ins:
        c.start()
    for c, then in zip(ins, outs):
        c.wait()
        for d in then:
            d.start()
    for then in outs:
        for d in then:
            d.wait()


def body(query, dec_query, cache_kv, span_kv, dec_kv, cache_fill, owner, slot, dec_len, w_uk, w_uv):
    vmem = pl.BlockSpec(memory_space=pltpu.VMEM)
    smem = pl.BlockSpec(memory_space=pltpu.SMEM)
    hbm = pl.BlockSpec(memory_space=pl.ANY)
    dma = pltpu.SemaphoreType.DMA
    shape = jax.ShapeDtypeStruct
    out, new_cache = pl.pallas_call(
        kernel,
        out_shape=(shape((COUNT, HEADS * DV), BF16), shape((KEY, POS), BF16)),
        in_specs=[hbm, hbm, hbm, hbm, hbm, smem, vmem, vmem, smem, hbm, hbm],
        out_specs=(vmem, hbm),
        scratch_shapes=[
            pltpu.VMEM(query.shape, BF16),
            pltpu.VMEM(dec_query.shape, BF16),
            pltpu.VMEM(span_kv.shape, BF16),
            pltpu.VMEM(dec_kv.shape, BF16),
            pltpu.VMEM((SEQ, SPAN // SEQ, SLICE), BF16),
            pltpu.VMEM((SEQ, ROWS // SEQ, SLICE), BF16),
            pltpu.VMEM((SEQ, SPAN // SEQ, KEY), BF16),
            pltpu.VMEM((SEQ, ROWS // SEQ, KEY), BF16),
            pltpu.VMEM((COUNT, SLICE), F32),
            pltpu.VMEM((COUNT, WIDE), F32),
            pltpu.VMEM((2 * SIDE, BAND, WIDE), BF16),
            pltpu.VMEM((2 * SIDE, BAND // 2, 128), BF16),
            pltpu.VMEM((2 * SIDE, WIDE, HALF), BF16),
            pltpu.VMEM((128, WIDE), BF16),
            pltpu.VMEM((HEADS, DN, DC), BF16),
            pltpu.VMEM((HEADS, DC, DV), BF16),
            pltpu.VMEM((KEY, POS), BF16),
            pltpu.VMEM((2 * SIDE, BAND, DC), F32),
            pltpu.VMEM((2 * SIDE, BAND, 1), F32),
            pltpu.VMEM((2 * SIDE, BAND, 1), F32),
            pltpu.VMEM((BAND, POS), F32),
            pltpu.VMEM((BAND, POS), F32),
            pltpu.VMEM((BAND, 128), F32),
            pltpu.VMEM((BAND, 128), F32),
            pltpu.VMEM((BAND, POS), BF16),
            pltpu.VMEM((6, BAND, DC), BF16),
            pltpu.VMEM((6, 8, 128), F32),
            pltpu.VMEM((6, BAND, DC), BF16),
            pltpu.VMEM((6, 8, 128), F32),
            dma((9,)),
            dma((4 * (SEQ - 1),)),
            dma((4 * (SEQ - 1),)),
            dma((6,)),
            dma((6,)),
            dma((12,)),
            dma((12,)),
            dma((12,)),
            dma((12,)),
        ],
        compiler_params=pltpu.CompilerParams(
            collective_id=0, has_side_effects=True, vmem_limit_bytes=56 * 2**20
        ),
        cost_estimate=pl.CostEstimate(
            flops=2 * STEPS * BAND * POS * (KEY + DC),
            bytes_accessed=8 * 2**20,
            transcendentals=STEPS * BAND * POS,
        ),
    )(
        query, dec_query, span_kv, dec_kv, cache_kv.T, cache_fill,
        owner.reshape(1, SPAN), slot.reshape(1, SPAN), dec_len, w_uk, w_uv,
    )
    span_out, dec_out, new_cache = pl.pallas_call(
        hand_over,
        out_shape=(
            shape((SPAN, HEADS * DV), BF16),
            shape((ROWS, HEADS * DV), BF16),
            shape((KEY, POS), BF16),
        ),
        in_specs=[hbm, hbm],
        out_specs=(hbm, hbm, hbm),
        scratch_shapes=[
            pltpu.VMEM((COUNT, HEADS * DV), BF16),
            pltpu.VMEM((KEY, POS), BF16),
            dma((7,)),
        ],
        compiler_params=pltpu.CompilerParams(vmem_limit_bytes=60 * 2**20),
        cost_estimate=pl.CostEstimate(flops=0, bytes_accessed=3 * 2**20, transcendentals=0),
    )(out, new_cache)
    return span_out, dec_out, new_cache.T


def solution(mesh):
    in_specs = (
        P(("grp", "seq"), None),
        P(("grp", "seq"), None),
        P(("grp", "seq"), None),
        P(("grp", "seq"), None),
        P(("grp", "seq"), None),
        P("grp"),
        P("grp"),
        P("grp"),
        P("grp"),
        P("seq", None, None),
        P("seq", None, None),
    )
    out_specs = (P("grp", "seq"), P("grp", "seq"), P(("grp", "seq"), None))
    return jax.shard_map(body, mesh=mesh, in_specs=in_specs, out_specs=out_specs, check_vma=False)
```

```python
import functools
import math

import jax
import jax.numpy as jnp
from jax import lax
from jax.experimental import pallas as pl
from jax.experimental.pallas import tpu as pltpu
from jax.sharding import PartitionSpec as P

MESH = pl.DeviceIdType.MESH
F32 = jnp.float32
BF16 = jnp.bfloat16

SIDE = 4
SEQ = SIDE * SIDE
HEADS = 8
DN = 128
DR = 64
DC = 512
DV = 128
KEY = DC + DR
WIDE = DC + 128
POS = 1024
SPAN = 64
ROWS = 16
COUNT = SPAN + ROWS
BAND = HEADS // 2 * COUNT
SLICE = HEADS * (DN + DR)
CHUNK = 256

SCALE2 = 0.1353 * math.log2(math.e)
LOW = -1e30

PIECES = ((0, 0), (0, 1), (1, 0), (3, 1), (1, 1), (3, 0), (2, 0), (2, 1))
HALF = POS // 2
ORDER_BAND = (0, 1, 2, 7, 0, 1, 2, 7, 3, 6, 3, 6, 4, 5, 4, 5) + (4, 5, 3, 6, 2, 7) * 2 + (0, 1) * 2
ORDER_KEYS = (0, 0, 0, 0, 1, 1, 1, 1) + (0, 0, 1, 1) * 2 + (2,) * 6 + (3,) * 6 + (2, 2, 3, 3)
STEPS = len(ORDER_BAND)
FINISH = 22


def dot(a, b):
    return jnp.dot(a, b, preferred_element_type=F32)


def dot_t(a, b):
    return lax.dot_general(a, b, (((1,), (1,)), ((), ())), preferred_element_type=F32)


def lane_mask(shape):
    return lax.broadcasted_iota(jnp.int32, shape, len(shape) - 1) < DR


def doubled():
    row = lax.broadcasted_iota(jnp.int32, (128, 128), 0)
    col = lax.broadcasted_iota(jnp.int32, (128, 128), 1)
    return jnp.where(row == lax.rem(col, DR), 1.0, 0.0).astype(BF16)


def pick(table, i):
    word = None
    for lo in reversed(range(0, len(table), 8)):
        packed = sum(entry << (4 * at) for at, entry in enumerate(table[lo : lo + 8]))
        word = jnp.int32(packed) if word is None else jnp.where(i < lo + 8, jnp.int32(packed), word)
    return lax.shift_right_logical(word, 4 * lax.rem(i, 8)) & 7


def kernel(
    query_hbm, dec_query_hbm, span_kv_hbm, dec_kv_hbm, cache_ref, fill_ref, owner_ref, slot_ref, dlen_ref,
    uk_hbm, uv_hbm,
    out_ref, newc_hbm,
    query_ref, dec_query_ref, span_kv_ref, dec_kv_ref, q_in, dq_in, kv_in, dkv_in, q_rows, kv_rows32, q_all, qr_all, k_all, k_own, uk, uv, newc,
    acc, peak, total, score_a, score_b, best_a, best_b, weights, o_send, e_send, o_recv, e_recv,
    local_sem, a_send, a_recv, c_send, c_recv, h_send, h_recv, p_send, p_recv,
):
    seq, grp = lax.axis_index("seq"), lax.axis_index("grp")
    core = lax.rem(grp, 2)
    z, x = seq // SIDE, lax.rem(seq, SIDE)

    def along_z(d):
        return lax.rem(z + d + SIDE, SIDE) * SIDE + x

    def along_x(d):
        return z * SIDE + lax.rem(x + d + SIDE, SIDE)

    def cache_peer(d):
        return (1 - core) * along_z(d) + core * along_x(d)

    def head_peer(d):
        return core * along_z(d) + (1 - core) * along_x(d)

    def remote(src, dst, send, recv, peer):
        return pltpu.make_async_remote_copy(
            src_ref=src, dst_ref=dst, send_sem=send, recv_sem=recv,
            device_id=(peer, grp), device_id_type=MESH,
        )

    barrier = pltpu.get_barrier_semaphore()
    for d in range(1, SEQ):
        pl.semaphore_signal(
            barrier, inc=1, device_id=(lax.rem(seq + d, SEQ), grp), device_id_type=MESH
        )

    inputs = [
        pltpu.make_async_copy(query_hbm, query_ref, local_sem.at[5]),
        pltpu.make_async_copy(dec_query_hbm, dec_query_ref, local_sem.at[6]),
        pltpu.make_async_copy(span_kv_hbm, span_kv_ref, local_sem.at[7]),
        pltpu.make_async_copy(dec_kv_hbm, dec_kv_ref, local_sem.at[8]),
    ]
    for c in inputs:
        c.start()
    own_keys = [
        pltpu.make_async_copy(
            cache_ref.at[:, pl.ds(h * HALF, HALF)], k_all.at[h, pl.ds(0, KEY)], local_sem.at[4 * h]
        )
        for h in range(2)
    ]
    own_uk = pltpu.make_async_copy(uk_hbm, uk, local_sem.at[1])
    own_uv = pltpu.make_async_copy(uv_hbm, uv, local_sem.at[2])
    for c in own_keys:
        c.start()
    own_uk.start()
    own_uv.start()

    def heads_of(ref, device):
        return ref.at[:, pl.ds(pl.multiple_of(device * SLICE, 128), SLICE)]

    for c in inputs:
        c.wait()
    exchange, exchange_kv = [], []
    for d in range(1, SEQ):
        peer = lax.rem(seq + d, SEQ)
        moves = (
            (heads_of(query_ref, peer), q_in, exchange),
            (heads_of(dec_query_ref, peer), dq_in, exchange),
            (span_kv_ref, kv_in, exchange_kv),
            (dec_kv_ref, dkv_in, exchange_kv),
        )
        for at, (src, dst, group) in enumerate(moves):
            i = (SEQ - 1) * at + d - 1
            group.append(remote(src, dst.at[seq], a_send.at[i], a_recv.at[i], peer))

    def ring(halves, send, recv, peer_of):
        count = len(halves(0, 0))

        def pair(i, src_slot, dst_slot, h, peer):
            src, dst = halves(src_slot, h), halves(dst_slot, h)
            return [
                remote(src[k], dst[k], send.at[count * i + k], recv.at[count * i + k], peer)
                for k in range(count)
            ]

        up, down = peer_of(1), peer_of(-1)
        first_up = pair(0, 0, 1, 0, up)
        first_down = pair(1, 0, 3, 1, down)
        second_up = pair(2, 0, 1, 1, up)
        second_down = pair(3, 0, 3, 0, down)
        onward_up = pair(4, 1, 2, 0, up)
        onward_down = pair(5, 3, 2, 1, down)
        return first_up, first_down, second_up, second_down, onward_up, onward_down

    def key_half(slot, h):
        return [k_all.at[PIECES.index((slot, h)), pl.ds(0, KEY)]]

    def query_half(slot, h):
        return [q_all.at[2 * slot + h, pl.ds(0, BAND), pl.ds(0, DC)], qr_all.at[2 * slot + h]]

    def start(*groups):
        for g in groups:
            for c in g:
                c.start()

    def arrived(*groups):
        for g in groups:
            for c in g:
                c.wait_recv()

    def sent(*groups):
        for g in groups:
            for c in g:
                c.wait_send()

    cring = ring(key_half, c_send, c_recv, cache_peer)
    hring = ring(query_half, h_send, h_recv, head_peer)

    def unpack_keys(block):
        for piece in (2 * block, 2 * block + 1):
            k_all[piece, KEY:WIDE, :] = k_all[piece, DC:KEY, :]

    def unpack_queries(band):
        for p in range(HEADS // 4):
            both = qr_all[band, COUNT * p : COUNT * (p + 1), :].astype(F32)
            mask = lane_mask(both.shape)
            at = 2 * COUNT * p
            q_all[band, at : at + COUNT, DC:WIDE] = jnp.where(mask, both, 0.0).astype(BF16)
            q_all[band, at + COUNT : at + 2 * COUNT, DC:WIDE] = jnp.where(mask, 0.0, both).astype(BF16)

    for c in own_keys:
        c.wait()
    mine = pl.ds(pl.multiple_of(seq * SLICE, 128), SLICE)
    q_in[seq] = query_ref[:, mine]
    dq_in[seq] = dec_query_ref[:, mine]
    kv_in[seq] = span_kv_ref[...]
    dkv_in[seq] = dec_kv_ref[...]
    unpack_keys(0)
    peak[...] = jnp.full(peak.shape, LOW, F32)
    total[...] = jnp.zeros(total.shape, F32)
    acc[...] = jnp.zeros(acc.shape, F32)
    e_send[...] = jnp.zeros(e_send.shape, F32)

    pl.semaphore_wait(barrier, SEQ - 1)
    for c in exchange[0::2] + exchange[1::2]:
        c.start()
    for c in exchange_kv[0::2] + exchange_kv[1::2]:
        c.start()
    start(cring[0], cring[1])

    own_uk.wait()
    for c in exchange:
        c.wait_recv()
    fours = SPAN // SEQ
    for device in range(SEQ):
        q_rows[fours * device : fours * (device + 1), :] = q_in[device].astype(F32)
        q_rows[SPAN + device : SPAN + device + 1, :] = dq_in[device].astype(F32)
    got = q_rows[...]
    for p in range(HEADS // 2):
        at = 3 * 128 * p
        t0, t1, t2 = (got[:, at + 128 * i : at + 128 * (i + 1)] for i in range(3))
        mask = lane_mask(t0.shape)
        nope = t0.astype(BF16)
        swapped = jnp.where(mask, t2, t1).astype(BF16)
        band, pair = p // 2, p % 2
        qr_all[band, COUNT * pair : COUNT * (pair + 1), :] = jnp.where(mask, t1, t2).astype(BF16)
        weight = uk[2 * p + 1]
        weight = jnp.concatenate([weight[DR:], weight[:DR]], axis=0)
        row0 = 2 * COUNT * pair
        q_all[band, row0 : row0 + COUNT, 0:DC] = dot(nope, uk[2 * p]).astype(BF16)
        q_all[band, row0 + COUNT : row0 + 2 * COUNT, 0:DC] = dot(swapped, weight).astype(BF16)
        if p == 1:
            start(hring[0])
        if p == 3:
            start(hring[1], hring[2], hring[3])
    unpack_queries(0)
    unpack_queries(1)

    for c in exchange_kv:
        c.wait_recv()
    kv_rows32[...] = jnp.zeros(kv_rows32.shape, F32)
    for device in range(SEQ):
        kv_rows32[fours * device : fours * (device + 1), 0:KEY] = kv_in[device].astype(F32)
        kv_rows32[SPAN + device : SPAN + device + 1, 0:KEY] = dkv_in[device].astype(F32)
    kv_rows = kv_rows32[...].astype(BF16)
    k_own[...] = jnp.zeros(k_own.shape, BF16)
    k_own[0:COUNT, 0:DC] = kv_rows[:, 0:DC]
    k_own[0:COUNT, DC:WIDE] = dot(kv_rows[:, DC:WIDE], doubled()).astype(BF16)

    def scores(band, block, out, best):
        top = None
        for side in range(2):
            slot = pick([PIECES[2 * b + side][0] for b in range(SIDE)], block)
            half = pick([PIECES[2 * b + side][1] for b in range(SIDE)], block)
            fill = fill_ref[cache_peer(-slot)] - half * HALF
            for j in range(0, HALF, CHUNK):
                s = dot(q_all[band], k_all[2 * block + side, :, j : j + CHUNK])
                local = lax.broadcasted_iota(jnp.int32, (1, CHUNK), 1) + j
                s = jnp.where(local < fill, s, LOW)
                out[:, side * HALF + j : side * HALF + j + CHUNK] = s
                for u in range(0, CHUNK, 128):
                    top = s[:, u : u + 128] if top is None else jnp.maximum(top, s[:, u : u + 128])
                yield
        best[...] = top

    def attend(band, block, now, later, ahead):
        score, best = now
        old = peak[band]
        top = jnp.maximum(old, jnp.max(best[...], axis=1, keepdims=True))
        keep = jnp.exp2((old - top) * SCALE2)
        add = None
        nxt = scores(*ahead, *later) if ahead is not None else iter((None,) * 4)
        for j in range(POS // CHUNK):
            next(nxt)
            at = slice(j * CHUNK, (j + 1) * CHUNK)
            e = jnp.exp2((score[:, at] - top) * SCALE2)
            weights[:, at] = e.astype(BF16)
            for u in range(0, CHUNK, 128):
                add = e[:, u : u + 128] if add is None else add + e[:, u : u + 128]
        next(nxt, None)
        out = dot_t(weights[:, 0:HALF], k_all[2 * block, 0:DC, :])
        out += dot_t(weights[:, HALF:POS], k_all[2 * block + 1, 0:DC, :])
        peak[band] = top
        total[band] = total[band] * keep + jnp.sum(add, axis=1, keepdims=True)
        acc[band] = acc[band] * keep + out

    eye = lax.broadcasted_iota(jnp.int32, (64, 128), 0) == lax.broadcasted_iota(jnp.int32, (64, 128), 1)

    def rows_to_lanes(level, ref, index):
        for i in range(BAND // 64):
            square = jnp.broadcast_to(level[64 * i : 64 * (i + 1)], (64, 128))
            ref[index, i : i + 1, :] = jnp.sum(jnp.where(eye, square, 0.0), axis=0, keepdims=True)

    def lanes_to_rows(ref, index):
        column = []
        for i in range(BAND // 64):
            square = jnp.broadcast_to(ref[index, i : i + 1, :], (64, 128))
            column.append(jnp.sum(jnp.where(eye, square, 0.0), axis=1, keepdims=True))
        return jnp.concatenate(column, axis=0)

    def back(band):
        peer, i = head_peer(jnp.where(band <= 4, -1, 1)), band - 2
        return [
            remote(o_send.at[i], o_recv.at[i], p_send.at[2 * i], p_recv.at[2 * i], peer),
            remote(e_send.at[i], e_recv.at[i], p_send.at[2 * i + 1], p_recv.at[2 * i + 1], peer),
        ]

    def finish(band):
        t = total[band]
        o_send[band - 2] = (acc[band] * (1.0 / t)).astype(BF16)
        rows_to_lanes(peak[band] * SCALE2 + jnp.log2(t), e_send, band - 2)

    def finish_both(band, other):
        arrived(back(other))
        t = total[band]
        here, there = peak[band] * SCALE2 + jnp.log2(t), lanes_to_rows(e_recv, other - 2)
        top = jnp.maximum(here, there)
        w_here, w_there = jnp.exp2(here - top), jnp.exp2(there - top)
        both = w_here + w_there
        norm = 1.0 / both
        part = acc[band] * (w_here * norm / t) + o_recv[other - 2].astype(F32) * (w_there * norm)
        o_send[band - 2] = part.astype(BF16)
        rows_to_lanes(top + jnp.log2(both), e_send, band - 2)

    qrow = lax.broadcasted_iota(jnp.int32, (COUNT, 128), 0)
    kcol = lax.broadcasted_iota(jnp.int32, (COUNT, 128), 1)
    limit = jnp.where(qrow < SPAN, qrow + 1, 0)
    for r in range(ROWS):
        limit = jnp.where(qrow == SPAN + r, dlen_ref[r], limit)
    seen = (kcol < limit) | ((qrow >= SPAN) & (kcol == qrow))
    hidden = jnp.where(seen, 0.0, 1.0)
    hidden = jnp.concatenate([hidden] * (HEADS // 2), axis=0)
    for band in range(2):
        s = jnp.where(hidden > 0.5, LOW, dot_t(q_all[band], k_own[...]))
        top = jnp.max(s, axis=1, keepdims=True)
        e = jnp.exp2((s - top) * SCALE2)
        peak[band] = top
        total[band] = jnp.sum(e, axis=1, keepdims=True)
        acc[band] = dot(e.astype(BF16), k_own[:, 0:DC])

    target = jnp.where(owner_ref[...] == seq, slot_ref[...], -1)
    span_rows = kv_rows[0:SPAN, 0:KEY]

    @pl.loop(0, POS // 256)
    def _(i):
        piece = i // 2
        local = lax.broadcasted_iota(jnp.int32, (256, SPAN), 0) + i * 256
        hot = jnp.where(local == target, 1.0, 0.0).astype(BF16)
        put = lax.dot_general(span_rows, hot, (((0,), (1,)), ((), ())), preferred_element_type=F32)
        any_hot = dot_t(jnp.ones((8, SPAN), BF16), hot)[0:1] > 0.5
        at = pl.ds(pl.multiple_of(lax.rem(i, 2) * 256, 256), 256)
        old = k_all[piece, 0:KEY, at].astype(F32)
        newc[:, pl.ds(pl.multiple_of(i * 256, 256), 256)] = jnp.where(any_hot, put, old).astype(BF16)

    put_cache = pltpu.make_async_copy(newc, newc_hbm, local_sem.at[3])
    put_cache.start()

    def event(g):
        @pl.when(g == 4)
        def _():
            arrived(cring[0], cring[1])
            unpack_keys(1)

        @pl.when(g == 2)
        def _():
            arrived(hring[0], hring[1])
            start(hring[4], hring[5])
            unpack_queries(2)
            unpack_queries(7)

        @pl.when(g == 8)
        def _():
            arrived(hring[2], hring[3])
            start(cring[2], cring[3])
            unpack_queries(3)
            unpack_queries(6)

        @pl.when(g == 12)
        def _():
            arrived(hring[4], hring[5])
            start(cring[4], cring[5])
            unpack_queries(4)
            unpack_queries(5)

        @pl.when(g == 16)
        def _():
            arrived(cring[2], cring[3])
            unpack_keys(2)

        @pl.when(g == 22)
        def _():
            arrived(cring[4], cring[5])
            unpack_keys(3)

        def leave(i):
            band = pick(ORDER_BAND, i)

            @pl.when(i < FINISH + 4)
            def _():
                finish(band)

            @pl.when(i >= FINISH + 4)
            def _():
                finish_both(band, jnp.where(band == 2, 4, 5))

            start(back(band))

        for late in (3, 2):
            i = g - late

            @pl.when((i >= FINISH) & (i < FINISH + 6) & ((late == 2) | (i > FINISH)))
            def _():
                leave(i)

    a, b = (score_a, best_a), (score_b, best_b)
    for _ in scores(0, 0, *a):
        pass

    def of(i):
        return pick(ORDER_BAND, i), pick(ORDER_KEYS, i)

    attend(0, 0, a, b, (ORDER_BAND[1], ORDER_KEYS[1]))

    @pl.loop(0, STEPS // 2 - 1)
    def _(j):
        i = 2 * j + 1
        g = i + 1

        @pl.when((g <= 4) | (g == 8) | (g == 12) | (g == 16) | (g >= FINISH))
        def _():
            event(g)

        attend(*of(i), b, a, of(i + 1))
        attend(*of(i + 1), a, b, of(i + 2))

    attend(ORDER_BAND[-1], ORDER_KEYS[-1], b, a, None)

    own_uv.wait()
    for half in range(2):
        parts = (half, 4 + half)
        levels = []
        for i in parts:
            arrived(back(i + 2))
            levels.append(lanes_to_rows(e_recv, i))
        own_level = peak[half] * SCALE2 + jnp.log2(total[half])
        top = own_level
        for level in levels:
            top = jnp.maximum(top, level)
        weight = jnp.exp2(own_level - top)
        shares = [jnp.exp2(level - top) for level in levels]
        norm = 1.0 / (weight + shares[0] + shares[1])
        first = weight * norm / total[half]
        shares = [share * norm for share in shares]
        for h in range(HEADS // 2):
            rows = slice(COUNT * h, COUNT * (h + 1))
            latent = acc[half, rows, :] * first[rows]
            for i, share in zip(parts, shares):
                latent = latent + o_recv[i, rows, :].astype(F32) * share[rows]
            head = HEADS // 2 * half + h
            value = dot(latent.astype(BF16), uv[head])
            out_ref[:, DV * head : DV * (head + 1)] = value.astype(BF16)

    put_cache.wait()
    for c in exchange + exchange_kv:
        c.wait_send()
    sent(*cring, *hring)
    for band in range(2, 2 * SIDE):
        sent(back(band))


def hand_over(out_ref, cache_ref, span_ref, dec_ref, new_ref, out, cache, sem):
    piece = KEY // 4
    ins = [pltpu.make_async_copy(out_ref, out, sem.at[0])]
    outs = [
        [
            pltpu.make_async_copy(out.at[pl.ds(0, SPAN)], span_ref, sem.at[5]),
            pltpu.make_async_copy(out.at[pl.ds(SPAN, ROWS)], dec_ref, sem.at[6]),
        ]
    ]
    for i in range(4):
        rows = pl.ds(i * piece, piece)
        ins.append(pltpu.make_async_copy(cache_ref.at[rows], cache.at[rows], sem.at[1 + i]))
        outs.append([pltpu.make_async_copy(cache.at[rows], new_ref.at[rows], sem.at[7 + i])])
    for c in ins:
        c.start()
    for c, then in zip(ins, outs):
        c.wait()
        for d in then:
            d.start()
    for then in outs:
        for d in then:
            d.wait()


def body(query, dec_query, cache_kv, span_kv, dec_kv, cache_fill, owner, slot, dec_len, w_uk, w_uv):
    vmem = pl.BlockSpec(memory_space=pltpu.VMEM)
    smem = pl.BlockSpec(memory_space=pltpu.SMEM)
    hbm = pl.BlockSpec(memory_space=pl.ANY)
    dma = pltpu.SemaphoreType.DMA
    shape = jax.ShapeDtypeStruct
    out, new_cache = pl.pallas_call(
        kernel,
        out_shape=(shape((COUNT, HEADS * DV), BF16), shape((KEY, POS), BF16)),
        in_specs=[hbm, hbm, hbm, hbm, hbm, smem, vmem, vmem, smem, hbm, hbm],
        out_specs=(vmem, hbm),
        scratch_shapes=[
            pltpu.VMEM(query.shape, BF16),
            pltpu.VMEM(dec_query.shape, BF16),
            pltpu.VMEM(span_kv.shape, BF16),
            pltpu.VMEM(dec_kv.shape, BF16),
            pltpu.VMEM((SEQ, SPAN // SEQ, SLICE), BF16),
            pltpu.VMEM((SEQ, ROWS // SEQ, SLICE), BF16),
            pltpu.VMEM((SEQ, SPAN // SEQ, KEY), BF16),
            pltpu.VMEM((SEQ, ROWS // SEQ, KEY), BF16),
            pltpu.VMEM((COUNT, SLICE), F32),
            pltpu.VMEM((COUNT, WIDE), F32),
            pltpu.VMEM((2 * SIDE, BAND, WIDE), BF16),
            pltpu.VMEM((2 * SIDE, BAND // 2, 128), BF16),
            pltpu.VMEM((2 * SIDE, WIDE, HALF), BF16),
            pltpu.VMEM((128, WIDE), BF16),
            pltpu.VMEM((HEADS, DN, DC), BF16),
            pltpu.VMEM((HEADS, DC, DV), BF16),
            pltpu.VMEM((KEY, POS), BF16),
            pltpu.VMEM((2 * SIDE, BAND, DC), F32),
            pltpu.VMEM((2 * SIDE, BAND, 1), F32),
            pltpu.VMEM((2 * SIDE, BAND, 1), F32),
            pltpu.VMEM((BAND, POS), F32),
            pltpu.VMEM((BAND, POS), F32),
            pltpu.VMEM((BAND, 128), F32),
            pltpu.VMEM((BAND, 128), F32),
            pltpu.VMEM((BAND, POS), BF16),
            pltpu.VMEM((6, BAND, DC), BF16),
            pltpu.VMEM((6, 8, 128), F32),
            pltpu.VMEM((6, BAND, DC), BF16),
            pltpu.VMEM((6, 8, 128), F32),
            dma((9,)),
            dma((4 * (SEQ - 1),)),
            dma((4 * (SEQ - 1),)),
            dma((6,)),
            dma((6,)),
            dma((12,)),
            dma((12,)),
            dma((12,)),
            dma((12,)),
        ],
        compiler_params=pltpu.CompilerParams(
            collective_id=0, has_side_effects=True, vmem_limit_bytes=56 * 2**20
        ),
        cost_estimate=pl.CostEstimate(
            flops=2 * STEPS * BAND * POS * (KEY + DC),
            bytes_accessed=8 * 2**20,
            transcendentals=STEPS * BAND * POS,
        ),
    )(
        query, dec_query, span_kv, dec_kv, cache_kv.T, cache_fill,
        owner.reshape(1, SPAN), slot.reshape(1, SPAN), dec_len, w_uk, w_uv,
    )
    span_out, dec_out, new_cache = pl.pallas_call(
        hand_over,
        out_shape=(
            shape((SPAN, HEADS * DV), BF16),
            shape((ROWS, HEADS * DV), BF16),
            shape((KEY, POS), BF16),
        ),
        in_specs=[hbm, hbm],
        out_specs=(hbm, hbm, hbm),
        scratch_shapes=[
            pltpu.VMEM((COUNT, HEADS * DV), BF16),
            pltpu.VMEM((KEY, POS), BF16),
            dma((11,)),
        ],
        compiler_params=pltpu.CompilerParams(vmem_limit_bytes=60 * 2**20),
        cost_estimate=pl.CostEstimate(flops=0, bytes_accessed=3 * 2**20, transcendentals=0),
    )(out, new_cache)
    return span_out, dec_out, new_cache.T


def solution(mesh):
    in_specs = (
        P(("grp", "seq"), None),
        P(("grp", "seq"), None),
        P(("grp", "seq"), None),
        P(("grp", "seq"), None),
        P(("grp", "seq"), None),
        P("grp"),
        P("grp"),
        P("grp"),
        P("grp"),
        P("seq", None, None),
        P("seq", None, None),
    )
    out_specs = (P("grp", "seq"), P("grp", "seq"), P(("grp", "seq"), None))
    return jax.shard_map(body, mesh=mesh, in_specs=in_specs, out_specs=out_specs, check_vma=False)
```

```python
import functools
import math

import jax
import jax.numpy as jnp
from jax import lax
from jax.experimental import pallas as pl
from jax.experimental.pallas import tpu as pltpu
from jax.sharding import PartitionSpec as P

MESH = pl.DeviceIdType.MESH
F32 = jnp.float32
BF16 = jnp.bfloat16

SIDE = 4
SEQ = SIDE * SIDE
HEADS = 8
DN = 128
DR = 64
DC = 512
DV = 128
KEY = DC + DR
WIDE = DC + 128
POS = 1024
SPAN = 64
ROWS = 16
COUNT = SPAN + ROWS
BAND = HEADS // 2 * COUNT
SLICE = HEADS * (DN + DR)
CHUNK = 256

SCALE2 = 0.1353 * math.log2(math.e)
LOW = -1e30

PIECES = ((0, 0), (0, 1), (1, 0), (3, 1), (1, 1), (3, 0), (2, 0), (2, 1))
HALF = POS // 2
ORDER_BAND = (0, 1, 2, 7, 0, 1, 2, 7, 3, 6, 3, 6, 4, 5, 4, 5) + (4, 5, 3, 6, 2, 7) * 2 + (0, 1) * 2
ORDER_KEYS = (0, 0, 0, 0, 1, 1, 1, 1) + (0, 0, 1, 1) * 2 + (2,) * 6 + (3,) * 6 + (2, 2, 3, 3)
STEPS = len(ORDER_BAND)
FINISH = 22


def dot(a, b):
    return jnp.dot(a, b, preferred_element_type=F32)


def dot_t(a, b):
    return lax.dot_general(a, b, (((1,), (1,)), ((), ())), preferred_element_type=F32)


def lane_mask(shape):
    return lax.broadcasted_iota(jnp.int32, shape, len(shape) - 1) < DR


def doubled():
    row = lax.broadcasted_iota(jnp.int32, (128, 128), 0)
    col = lax.broadcasted_iota(jnp.int32, (128, 128), 1)
    return jnp.where(row == lax.rem(col, DR), 1.0, 0.0).astype(BF16)


def pick(table, i):
    word = None
    for lo in reversed(range(0, len(table), 8)):
        packed = sum(entry << (4 * at) for at, entry in enumerate(table[lo : lo + 8]))
        word = jnp.int32(packed) if word is None else jnp.where(i < lo + 8, jnp.int32(packed), word)
    return lax.shift_right_logical(word, 4 * lax.rem(i, 8)) & 7


def kernel(
    query_hbm, dec_query_hbm, span_kv_hbm, dec_kv_hbm, cache_ref, fill_ref, owner_ref, slot_ref, dlen_ref,
    uk_hbm, uv_hbm,
    out_ref, newc_hbm,
    query_ref, dec_query_ref, span_kv_ref, dec_kv_ref, q_in, dq_in, kv_in, dkv_in, q_rows, kv_rows32, q_all, qr_all, k_all, k_own, uk, uv, newc,
    acc, peak, total, score_a, score_b, best_a, best_b, weights, o_send, e_send, o_recv, e_recv,
    local_sem, a_send, a_recv, c_send, c_recv, h_send, h_recv, p_send, p_recv,
):
    seq, grp = lax.axis_index("seq"), lax.axis_index("grp")
    core = lax.rem(grp, 2)
    z, x = seq // SIDE, lax.rem(seq, SIDE)

    def along_z(d):
        return lax.rem(z + d + SIDE, SIDE) * SIDE + x

    def along_x(d):
        return z * SIDE + lax.rem(x + d + SIDE, SIDE)

    def cache_peer(d):
        return (1 - core) * along_z(d) + core * along_x(d)

    def head_peer(d):
        return core * along_z(d) + (1 - core) * along_x(d)

    def remote(src, dst, send, recv, peer):
        return pltpu.make_async_remote_copy(
            src_ref=src, dst_ref=dst, send_sem=send, recv_sem=recv,
            device_id=(peer, grp), device_id_type=MESH,
        )

    barrier = pltpu.get_barrier_semaphore()
    for d in range(1, SEQ):
        pl.semaphore_signal(
            barrier, inc=1, device_id=(lax.rem(seq + d, SEQ), grp), device_id_type=MESH
        )

    inputs = [
        pltpu.make_async_copy(query_hbm, query_ref, local_sem.at[5]),
        pltpu.make_async_copy(dec_query_hbm, dec_query_ref, local_sem.at[6]),
        pltpu.make_async_copy(span_kv_hbm, span_kv_ref, local_sem.at[7]),
        pltpu.make_async_copy(dec_kv_hbm, dec_kv_ref, local_sem.at[8]),
    ]
    for c in inputs:
        c.start()
    own_keys = [
        pltpu.make_async_copy(
            cache_ref.at[:, pl.ds(h * HALF, HALF)], k_all.at[h, pl.ds(0, KEY)], local_sem.at[4 * h]
        )
        for h in range(2)
    ]
    own_uk = pltpu.make_async_copy(uk_hbm, uk, local_sem.at[1])
    own_uv = pltpu.make_async_copy(uv_hbm, uv, local_sem.at[2])
    for c in own_keys:
        c.start()
    own_uk.start()
    own_uv.start()

    def heads_of(ref, device):
        return ref.at[:, pl.ds(pl.multiple_of(device * SLICE, 128), SLICE)]

    for c in inputs:
        c.wait()
    exchange, exchange_kv = [], []
    for d in range(1, SEQ):
        peer = lax.rem(seq + d, SEQ)
        moves = (
            (heads_of(query_ref, peer), q_in, exchange),
            (heads_of(dec_query_ref, peer), dq_in, exchange),
            (span_kv_ref, kv_in, exchange_kv),
            (dec_kv_ref, dkv_in, exchange_kv),
        )
        for at, (src, dst, group) in enumerate(moves):
            i = (SEQ - 1) * at + d - 1
            group.append(remote(src, dst.at[seq], a_send.at[i], a_recv.at[i], peer))

    def ring(halves, send, recv, peer_of):
        count = len(halves(0, 0))

        def pair(i, src_slot, dst_slot, h, peer):
            src, dst = halves(src_slot, h), halves(dst_slot, h)
            return [
                remote(src[k], dst[k], send.at[count * i + k], recv.at[count * i + k], peer)
                for k in range(count)
            ]

        up, down = peer_of(1), peer_of(-1)
        first_up = pair(0, 0, 1, 0, up)
        first_down = pair(1, 0, 3, 1, down)
        second_up = pair(2, 0, 1, 1, up)
        second_down = pair(3, 0, 3, 0, down)
        onward_up = pair(4, 1, 2, 0, up)
        onward_down = pair(5, 3, 2, 1, down)
        return first_up, first_down, second_up, second_down, onward_up, onward_down

    def key_half(slot, h):
        return [k_all.at[PIECES.index((slot, h)), pl.ds(0, KEY)]]

    def query_half(slot, h):
        return [q_all.at[2 * slot + h, pl.ds(0, BAND), pl.ds(0, DC)], qr_all.at[2 * slot + h]]

    def start(*groups):
        for g in groups:
            for c in g:
                c.start()

    def arrived(*groups):
        for g in groups:
            for c in g:
                c.wait_recv()

    def sent(*groups):
        for g in groups:
            for c in g:
                c.wait_send()

    cring = ring(key_half, c_send, c_recv, cache_peer)
    hring = ring(query_half, h_send, h_recv, head_peer)

    def unpack_keys(block):
        for piece in (2 * block, 2 * block + 1):
            k_all[piece, KEY:WIDE, :] = k_all[piece, DC:KEY, :]

    def unpack_queries(band):
        for p in range(HEADS // 4):
            both = qr_all[band, COUNT * p : COUNT * (p + 1), :].astype(F32)
            mask = lane_mask(both.shape)
            at = 2 * COUNT * p
            q_all[band, at : at + COUNT, DC:WIDE] = jnp.where(mask, both, 0.0).astype(BF16)
            q_all[band, at + COUNT : at + 2 * COUNT, DC:WIDE] = jnp.where(mask, 0.0, both).astype(BF16)

    for c in own_keys:
        c.wait()
    mine = pl.ds(pl.multiple_of(seq * SLICE, 128), SLICE)
    q_in[seq] = query_ref[:, mine]
    dq_in[seq] = dec_query_ref[:, mine]
    kv_in[seq] = span_kv_ref[...]
    dkv_in[seq] = dec_kv_ref[...]
    unpack_keys(0)
    peak[...] = jnp.full(peak.shape, LOW, F32)
    total[...] = jnp.zeros(total.shape, F32)
    acc[...] = jnp.zeros(acc.shape, F32)
    e_send[...] = jnp.zeros(e_send.shape, F32)

    pl.semaphore_wait(barrier, SEQ - 1)
    far = sorted(range(1, SEQ), key=lambda d: -min(d // SIDE, SIDE - d // SIDE) - min(d % SIDE, SIDE - d % SIDE))
    for first in range(2):
        for d in far:
            exchange[2 * (d - 1) + first].start()
    for c in exchange_kv[0::2] + exchange_kv[1::2]:
        c.start()
    start(cring[0], cring[1])

    own_uk.wait()
    for c in exchange:
        c.wait_recv()
    fours = SPAN // SEQ
    for device in range(SEQ):
        q_rows[fours * device : fours * (device + 1), :] = q_in[device].astype(F32)
        q_rows[SPAN + device : SPAN + device + 1, :] = dq_in[device].astype(F32)
    got = q_rows[...]
    for p in range(HEADS // 2):
        at = 3 * 128 * p
        t0, t1, t2 = (got[:, at + 128 * i : at + 128 * (i + 1)] for i in range(3))
        mask = lane_mask(t0.shape)
        nope = t0.astype(BF16)
        swapped = jnp.where(mask, t2, t1).astype(BF16)
        band, pair = p // 2, p % 2
        qr_all[band, COUNT * pair : COUNT * (pair + 1), :] = jnp.where(mask, t1, t2).astype(BF16)
        weight = uk[2 * p + 1]
        weight = jnp.concatenate([weight[DR:], weight[:DR]], axis=0)
        row0 = 2 * COUNT * pair
        q_all[band, row0 : row0 + COUNT, 0:DC] = dot(nope, uk[2 * p]).astype(BF16)
        q_all[band, row0 + COUNT : row0 + 2 * COUNT, 0:DC] = dot(swapped, weight).astype(BF16)
        if p == 1:
            start(hring[0])
        if p == 3:
            start(hring[1], hring[2], hring[3])
    unpack_queries(0)
    unpack_queries(1)

    for c in exchange_kv:
        c.wait_recv()
    kv_rows32[...] = jnp.zeros(kv_rows32.shape, F32)
    for device in range(SEQ):
        kv_rows32[fours * device : fours * (device + 1), 0:KEY] = kv_in[device].astype(F32)
        kv_rows32[SPAN + device : SPAN + device + 1, 0:KEY] = dkv_in[device].astype(F32)
    kv_rows = kv_rows32[...].astype(BF16)
    k_own[...] = jnp.zeros(k_own.shape, BF16)
    k_own[0:COUNT, 0:DC] = kv_rows[:, 0:DC]
    k_own[0:COUNT, DC:WIDE] = dot(kv_rows[:, DC:WIDE], doubled()).astype(BF16)

    def scores(band, block, out, best):
        top = None
        for side in range(2):
            slot = pick([PIECES[2 * b + side][0] for b in range(SIDE)], block)
            half = pick([PIECES[2 * b + side][1] for b in range(SIDE)], block)
            fill = fill_ref[cache_peer(-slot)] - half * HALF
            for j in range(0, HALF, CHUNK):
                s = dot(q_all[band], k_all[2 * block + side, :, j : j + CHUNK])
                local = lax.broadcasted_iota(jnp.int32, (1, CHUNK), 1) + j
                s = jnp.where(local < fill, s, LOW)
                out[:, side * HALF + j : side * HALF + j + CHUNK] = s
                for u in range(0, CHUNK, 128):
                    top = s[:, u : u + 128] if top is None else jnp.maximum(top, s[:, u : u + 128])
                yield
        best[...] = top

    def attend(band, block, now, later, ahead):
        score, best = now
        old = peak[band]
        top = jnp.maximum(old, jnp.max(best[...], axis=1, keepdims=True))
        keep = jnp.exp2((old - top) * SCALE2)
        add = None
        nxt = scores(*ahead, *later) if ahead is not None else iter((None,) * 4)
        for j in range(POS // CHUNK):
            next(nxt)
            at = slice(j * CHUNK, (j + 1) * CHUNK)
            e = jnp.exp2((score[:, at] - top) * SCALE2)
            weights[:, at] = e.astype(BF16)
            for u in range(0, CHUNK, 128):
                add = e[:, u : u + 128] if add is None else add + e[:, u : u + 128]
        next(nxt, None)
        out = dot_t(weights[:, 0:HALF], k_all[2 * block, 0:DC, :])
        out += dot_t(weights[:, HALF:POS], k_all[2 * block + 1, 0:DC, :])
        peak[band] = top
        total[band] = total[band] * keep + jnp.sum(add, axis=1, keepdims=True)
        acc[band] = acc[band] * keep + out

    eye = lax.broadcasted_iota(jnp.int32, (64, 128), 0) == lax.broadcasted_iota(jnp.int32, (64, 128), 1)

    def rows_to_lanes(level, ref, index):
        for i in range(BAND // 64):
            square = jnp.broadcast_to(level[64 * i : 64 * (i + 1)], (64, 128))
            ref[index, i : i + 1, :] = jnp.sum(jnp.where(eye, square, 0.0), axis=0, keepdims=True)

    def lanes_to_rows(ref, index):
        column = []
        for i in range(BAND // 64):
            square = jnp.broadcast_to(ref[index, i : i + 1, :], (64, 128))
            column.append(jnp.sum(jnp.where(eye, square, 0.0), axis=1, keepdims=True))
        return jnp.concatenate(column, axis=0)

    def back(band):
        peer, i = head_peer(jnp.where(band <= 4, -1, 1)), band - 2
        return [
            remote(o_send.at[i], o_recv.at[i], p_send.at[2 * i], p_recv.at[2 * i], peer),
            remote(e_send.at[i], e_recv.at[i], p_send.at[2 * i + 1], p_recv.at[2 * i + 1], peer),
        ]

    def finish(band):
        t = total[band]
        o_send[band - 2] = (acc[band] * (1.0 / t)).astype(BF16)
        rows_to_lanes(peak[band] * SCALE2 + jnp.log2(t), e_send, band - 2)

    def finish_both(band, other):
        arrived(back(other))
        t = total[band]
        here, there = peak[band] * SCALE2 + jnp.log2(t), lanes_to_rows(e_recv, other - 2)
        top = jnp.maximum(here, there)
        w_here, w_there = jnp.exp2(here - top), jnp.exp2(there - top)
        both = w_here + w_there
        norm = 1.0 / both
        part = acc[band] * (w_here * norm / t) + o_recv[other - 2].astype(F32) * (w_there * norm)
        o_send[band - 2] = part.astype(BF16)
        rows_to_lanes(top + jnp.log2(both), e_send, band - 2)

    qrow = lax.broadcasted_iota(jnp.int32, (COUNT, 128), 0)
    kcol = lax.broadcasted_iota(jnp.int32, (COUNT, 128), 1)
    limit = jnp.where(qrow < SPAN, qrow + 1, 0)
    for r in range(ROWS):
        limit = jnp.where(qrow == SPAN + r, dlen_ref[r], limit)
    seen = (kcol < limit) | ((qrow >= SPAN) & (kcol == qrow))
    hidden = jnp.where(seen, 0.0, 1.0)
    hidden = jnp.concatenate([hidden] * (HEADS // 2), axis=0)
    for band in range(2):
        s = jnp.where(hidden > 0.5, LOW, dot_t(q_all[band], k_own[...]))
        top = jnp.max(s, axis=1, keepdims=True)
        e = jnp.exp2((s - top) * SCALE2)
        peak[band] = top
        total[band] = jnp.sum(e, axis=1, keepdims=True)
        acc[band] = dot(e.astype(BF16), k_own[:, 0:DC])

    target = jnp.where(owner_ref[...] == seq, slot_ref[...], -1)
    span_rows = kv_rows[0:SPAN, 0:KEY]

    @pl.loop(0, POS // 256)
    def _(i):
        piece = i // 2
        local = lax.broadcasted_iota(jnp.int32, (256, SPAN), 0) + i * 256
        hot = jnp.where(local == target, 1.0, 0.0).astype(BF16)
        put = lax.dot_general(span_rows, hot, (((0,), (1,)), ((), ())), preferred_element_type=F32)
        any_hot = dot_t(jnp.ones((8, SPAN), BF16), hot)[0:1] > 0.5
        at = pl.ds(pl.multiple_of(lax.rem(i, 2) * 256, 256), 256)
        old = k_all[piece, 0:KEY, at].astype(F32)
        newc[:, pl.ds(pl.multiple_of(i * 256, 256), 256)] = jnp.where(any_hot, put, old).astype(BF16)

    put_cache = pltpu.make_async_copy(newc, newc_hbm, local_sem.at[3])
    put_cache.start()

    def event(g):
        @pl.when(g == 4)
        def _():
            arrived(cring[0], cring[1])
            unpack_keys(1)

        @pl.when(g == 2)
        def _():
            arrived(hring[0], hring[1])
            start(hring[4], hring[5])
            unpack_queries(2)
            unpack_queries(7)

        @pl.when(g == 8)
        def _():
            arrived(hring[2], hring[3])
            start(cring[2], cring[3])
            unpack_queries(3)
            unpack_queries(6)

        @pl.when(g == 12)
        def _():
            arrived(hring[4], hring[5])
            start(cring[4], cring[5])
            unpack_queries(4)
            unpack_queries(5)

        @pl.when(g == 16)
        def _():
            arrived(cring[2], cring[3])
            unpack_keys(2)

        @pl.when(g == 22)
        def _():
            arrived(cring[4], cring[5])
            unpack_keys(3)

        def leave(i):
            band = pick(ORDER_BAND, i)

            @pl.when(i < FINISH + 4)
            def _():
                finish(band)

            @pl.when(i >= FINISH + 4)
            def _():
                finish_both(band, jnp.where(band == 2, 4, 5))

            start(back(band))

        for late in (3, 2):
            i = g - late

            @pl.when((i >= FINISH) & (i < FINISH + 6) & ((late == 2) | (i > FINISH)))
            def _():
                leave(i)

    a, b = (score_a, best_a), (score_b, best_b)
    for _ in scores(0, 0, *a):
        pass

    def of(i):
        return pick(ORDER_BAND, i), pick(ORDER_KEYS, i)

    attend(0, 0, a, b, (ORDER_BAND[1], ORDER_KEYS[1]))

    @pl.loop(0, STEPS // 2 - 1)
    def _(j):
        i = 2 * j + 1
        g = i + 1

        @pl.when((g <= 4) | (g == 8) | (g == 12) | (g == 16) | (g >= FINISH))
        def _():
            event(g)

        attend(*of(i), b, a, of(i + 1))
        attend(*of(i + 1), a, b, of(i + 2))

    attend(ORDER_BAND[-1], ORDER_KEYS[-1], b, a, None)

    own_uv.wait()
    for half in range(2):
        parts = (half, 4 + half)
        levels = []
        for i in parts:
            arrived(back(i + 2))
            levels.append(lanes_to_rows(e_recv, i))
        own_level = peak[half] * SCALE2 + jnp.log2(total[half])
        top = own_level
        for level in levels:
            top = jnp.maximum(top, level)
        weight = jnp.exp2(own_level - top)
        shares = [jnp.exp2(level - top) for level in levels]
        norm = 1.0 / (weight + shares[0] + shares[1])
        first = weight * norm / total[half]
        shares = [share * norm for share in shares]
        for h in range(HEADS // 2):
            rows = slice(COUNT * h, COUNT * (h + 1))
            latent = acc[half, rows, :] * first[rows]
            for i, share in zip(parts, shares):
                latent = latent + o_recv[i, rows, :].astype(F32) * share[rows]
            head = HEADS // 2 * half + h
            value = dot(latent.astype(BF16), uv[head])
            out_ref[:, DV * head : DV * (head + 1)] = value.astype(BF16)

    put_cache.wait()
    for c in exchange + exchange_kv:
        c.wait_send()
    sent(*cring, *hring)
    for band in range(2, 2 * SIDE):
        sent(back(band))


def hand_over(out_ref, cache_ref, span_ref, dec_ref, new_ref, out, cache, sem):
    piece = KEY // 4
    ins = [pltpu.make_async_copy(out_ref, out, sem.at[0])]
    outs = [
        [
            pltpu.make_async_copy(out.at[pl.ds(0, SPAN)], span_ref, sem.at[5]),
            pltpu.make_async_copy(out.at[pl.ds(SPAN, ROWS)], dec_ref, sem.at[6]),
        ]
    ]
    for i in range(4):
        rows = pl.ds(i * piece, piece)
        ins.append(pltpu.make_async_copy(cache_ref.at[rows], cache.at[rows], sem.at[1 + i]))
        outs.append([pltpu.make_async_copy(cache.at[rows], new_ref.at[rows], sem.at[7 + i])])
    for c in ins:
        c.start()
    for c, then in zip(ins, outs):
        c.wait()
        for d in then:
            d.start()
    for then in outs:
        for d in then:
            d.wait()


def body(query, dec_query, cache_kv, span_kv, dec_kv, cache_fill, owner, slot, dec_len, w_uk, w_uv):
    vmem = pl.BlockSpec(memory_space=pltpu.VMEM)
    smem = pl.BlockSpec(memory_space=pltpu.SMEM)
    hbm = pl.BlockSpec(memory_space=pl.ANY)
    dma = pltpu.SemaphoreType.DMA
    shape = jax.ShapeDtypeStruct
    out, new_cache = pl.pallas_call(
        kernel,
        out_shape=(shape((COUNT, HEADS * DV), BF16), shape((KEY, POS), BF16)),
        in_specs=[hbm, hbm, hbm, hbm, hbm, smem, vmem, vmem, smem, hbm, hbm],
        out_specs=(vmem, hbm),
        scratch_shapes=[
            pltpu.VMEM(query.shape, BF16),
            pltpu.VMEM(dec_query.shape, BF16),
            pltpu.VMEM(span_kv.shape, BF16),
            pltpu.VMEM(dec_kv.shape, BF16),
            pltpu.VMEM((SEQ, SPAN // SEQ, SLICE), BF16),
            pltpu.VMEM((SEQ, ROWS // SEQ, SLICE), BF16),
            pltpu.VMEM((SEQ, SPAN // SEQ, KEY), BF16),
            pltpu.VMEM((SEQ, ROWS // SEQ, KEY), BF16),
            pltpu.VMEM((COUNT, SLICE), F32),
            pltpu.VMEM((COUNT, WIDE), F32),
            pltpu.VMEM((2 * SIDE, BAND, WIDE), BF16),
            pltpu.VMEM((2 * SIDE, BAND // 2, 128), BF16),
            pltpu.VMEM((2 * SIDE, WIDE, HALF), BF16),
            pltpu.VMEM((128, WIDE), BF16),
            pltpu.VMEM((HEADS, DN, DC), BF16),
            pltpu.VMEM((HEADS, DC, DV), BF16),
            pltpu.VMEM((KEY, POS), BF16),
            pltpu.VMEM((2 * SIDE, BAND, DC), F32),
            pltpu.VMEM((2 * SIDE, BAND, 1), F32),
            pltpu.VMEM((2 * SIDE, BAND, 1), F32),
            pltpu.VMEM((BAND, POS), F32),
            pltpu.VMEM((BAND, POS), F32),
            pltpu.VMEM((BAND, 128), F32),
            pltpu.VMEM((BAND, 128), F32),
            pltpu.VMEM((BAND, POS), BF16),
            pltpu.VMEM((6, BAND, DC), BF16),
            pltpu.VMEM((6, 8, 128), F32),
            pltpu.VMEM((6, BAND, DC), BF16),
            pltpu.VMEM((6, 8, 128), F32),
            dma((9,)),
            dma((4 * (SEQ - 1),)),
            dma((4 * (SEQ - 1),)),
            dma((6,)),
            dma((6,)),
            dma((12,)),
            dma((12,)),
            dma((12,)),
            dma((12,)),
        ],
        compiler_params=pltpu.CompilerParams(
            collective_id=0, has_side_effects=True, vmem_limit_bytes=56 * 2**20
        ),
        cost_estimate=pl.CostEstimate(
            flops=2 * STEPS * BAND * POS * (KEY + DC),
            bytes_accessed=8 * 2**20,
            transcendentals=STEPS * BAND * POS,
        ),
    )(
        query, dec_query, span_kv, dec_kv, cache_kv.T, cache_fill,
        owner.reshape(1, SPAN), slot.reshape(1, SPAN), dec_len, w_uk, w_uv,
    )
    span_out, dec_out, new_cache = pl.pallas_call(
        hand_over,
        out_shape=(
            shape((SPAN, HEADS * DV), BF16),
            shape((ROWS, HEADS * DV), BF16),
            shape((KEY, POS), BF16),
        ),
        in_specs=[hbm, hbm],
        out_specs=(hbm, hbm, hbm),
        scratch_shapes=[
            pltpu.VMEM((COUNT, HEADS * DV), BF16),
            pltpu.VMEM((KEY, POS), BF16),
            dma((11,)),
        ],
        compiler_params=pltpu.CompilerParams(vmem_limit_bytes=60 * 2**20),
        cost_estimate=pl.CostEstimate(flops=0, bytes_accessed=3 * 2**20, transcendentals=0),
    )(out, new_cache)
    return span_out, dec_out, new_cache.T


def solution(mesh):
    in_specs = (
        P(("grp", "seq"), None),
        P(("grp", "seq"), None),
        P(("grp", "seq"), None),
        P(("grp", "seq"), None),
        P(("grp", "seq"), None),
        P("grp"),
        P("grp"),
        P("grp"),
        P("grp"),
        P("seq", None, None),
        P("seq", None, None),
    )
    out_specs = (P("grp", "seq"), P("grp", "seq"), P(("grp", "seq"), None))
    return jax.shard_map(body, mesh=mesh, in_specs=in_specs, out_specs=out_specs, check_vma=False)
```
